32 devices in a mesh: dom: 8 (over y, x, core), rot: 4 (over z).
Axes of the slice: x: 2, y: 2, z: 4, core: 2. Of those that a mesh axis runs over, the one named last changes fastest.
Arguments:
- particles: bfloat16 [512, 8192], P('dom'), may hold values from -8 to 8, as said below
- assign: int32 [512], P('dom'), may hold values from 0 to 47, as said below
- rot_index: int32 [512], P('dom'), may hold values from 0 to 31
- group: int32 [512], P('dom'), may hold values from 0 to 31
- ctf_table: float32 [32, 64], replicated, may hold values from -1 to 1
Outputs:
- refs: bfloat16 [48, 8192], P('dom')
- best_scores: float32 [512, 48], P(('dom', 'rot'))
The draws below stay inside these ranges and needn't reach their ends.
Inputs may be any that keep to these rules, and one draw needn't show every extreme that they name: `particles`: rows in custom order; values real. `assign`: owner o holds classes o * 6 to o * 6 + 5. The 64 particles of one index of dom form 4 shares of 16 consecutive particles; within each share at most 4 particles are assigned to the classes of one owner.
All inputs are finite; a program needn't handle non-finite values.
Results may differ from the reference program's by a relative error of at most 0.0027.
Values may be sent and summed in bfloat16 or wider, within the bound.
A program may use at most 128 MiB of HBM per device.

```python
import math
import jax
import jax.numpy as jnp
from jax import lax

CYCLES = 64
MFREQ = 64
CLS_DEV = 6
GROUPS = 32
P_DEV = 64
K = 8192
CLASSES = 48
ROT = 32
PARTICLES = 512
SHARE = 16
CAP = 4
N_DOM = 8
N_ROT = 4


def draw_particles(key, part):
    base_key = jax.random.fold_in(key, 7)
    key_column, key_values = jax.random.split(base_key, 2)
    column = jnp.exp(jax.random.uniform(key_column, (K,), jnp.float32, 0.0, math.log(10.0))) / math.sqrt(10.0)
    values = jax.random.normal(key_values, (PARTICLES, K), jnp.float32) * column[None, :]
    return jnp.clip(values, -8.0, 8.0).astype(jnp.bfloat16)


def shuffled_slots(one_key):
    return jax.random.permutation(one_key, (N_DOM - 1) * (CAP - 1))


def shuffled_rows(one_key):
    return jax.random.permutation(one_key, SHARE)


def draw_assign(key, part):
    base_key = jax.random.fold_in(key, 13)
    key_hot, key_slots, key_order, key_within = jax.random.split(base_key, 4)
    blocks = PARTICLES // SHARE
    hot = jax.random.randint(key_hot, (N_ROT,), 0, N_DOM)
    hot_rows = hot[jnp.arange(blocks) % N_ROT]
    picks = jax.vmap(shuffled_slots)(jax.random.split(key_slots, blocks))[:, :SHARE - CAP]
    others = (hot_rows[:, None] + 1 + picks // (CAP - 1)) % N_DOM
    owners = jnp.concatenate([jnp.broadcast_to(hot_rows[:, None], (blocks, CAP)), others], axis=1)
    order = jax.vmap(shuffled_rows)(jax.random.split(key_order, blocks))
    owners = jnp.take_along_axis(owners, order, axis=1)
    within = jax.random.randint(key_within, (blocks, SHARE), 0, CLS_DEV)
    return (owners * CLS_DEV + within).reshape(PARTICLES).astype(jnp.int32)


def plant(result, own_key, low, largest):
    longest = result.shape.index(max(result.shape))
    spots = []
    for shift in (0, 1):
        where = [jax.random.randint(jax.random.fold_in(own_key, axis), (), 0, length) for axis, length in enumerate(result.shape)]
        where[longest] = (where[longest] + shift) % result.shape[longest]
        spots.append(tuple(where))
    return result.at[spots[0]].set(low).at[spots[1]].set(largest)


def setup_inputs(seed: int = 0) -> dict:
    keys = jax.random.split(jax.random.key(seed), 6)
    return {
        "particles": draw_particles(jax.random.fold_in(keys[5], 71), 0),
        "assign": draw_assign(jax.random.fold_in(keys[5], 71), 0),
        "rot_index": plant(jax.random.randint(keys[2], (PARTICLES,), 0, ROT), jax.random.fold_in(keys[2], 1), 0, ROT - 1).astype(jnp.int32),
        "group": plant(jax.random.randint(keys[3], (PARTICLES,), 0, GROUPS), jax.random.fold_in(keys[3], 1), 0, GROUPS - 1).astype(jnp.int32),
        "ctf_table": jnp.clip(jax.random.uniform(keys[4], (GROUPS, CYCLES), jnp.float32, -1.0, 1.0), -1.0, 1.0),
    }


def angles(index, total):
    freqs = jnp.arange(MFREQ, dtype=jnp.int32)
    phase = freqs[None, :] * index[:, None] % total
    return phase.astype(jnp.float32) * (2.0 * math.pi / total)

def derotate(spec, rotation, ctf_rows, total):
    count = spec.shape[0]
    layered = spec.reshape(count, 2, CYCLES, MFREQ)
    real_part = layered[:, 0]
    imag_part = layered[:, 1]
    angle = angles(rotation, total)
    cosine = jnp.cos(angle)[:, None, :]
    sine = jnp.sin(angle)[:, None, :]
    turned = jnp.stack([real_part * cosine + imag_part * sine, imag_part * cosine - real_part * sine], axis=1)
    return (turned * ctf_rows[:, None, :, None]).reshape(count, K)

def rotate_refs(refs, rotation, total):
    count = refs.shape[0]
    layered = refs.astype(jnp.float32).reshape(count, 2, CYCLES, MFREQ)
    real_part = layered[:, 0]
    imag_part = layered[:, 1]
    angle = angles(jnp.reshape(rotation, (1,)).astype(jnp.int32), total)
    cosine = jnp.cos(angle)
    sine = jnp.sin(angle)
    turned = jnp.stack([real_part * cosine - imag_part * sine, real_part * sine + imag_part * cosine], axis=1)
    return turned.reshape(count, K).astype(jnp.bfloat16)

def reference(particles, assign, rot_index, group, ctf_table):
    ctf_rows = ctf_table[group]

    def absorb(carry, block_index):
        numer, denom = carry
        first = (block_index * P_DEV).astype(jnp.int32)
        rows = lax.dynamic_slice_in_dim(particles, first, P_DEV, 0).astype(jnp.float32)
        labels = lax.dynamic_slice_in_dim(assign, first, P_DEV, 0)
        turns = lax.dynamic_slice_in_dim(rot_index, first, P_DEV, 0)
        factors = lax.dynamic_slice_in_dim(ctf_rows, first, P_DEV, 0)
        weighted = derotate(rows, turns, factors, ROT)
        numer = numer + jax.ops.segment_sum(weighted, labels, num_segments=CLASSES)
        denom = denom + jax.ops.segment_sum(factors * factors, labels, num_segments=CLASSES)
        return ((numer, denom), None)
    start_carry = (jnp.zeros((CLASSES, K), jnp.float32), jnp.zeros((CLASSES, CYCLES), jnp.float32))
    (numer, denom), _ = lax.scan(absorb, start_carry, jnp.arange(PARTICLES // P_DEV, dtype=jnp.int32))
    plain = numer.reshape(CLASSES, 2, CYCLES, MFREQ) / (denom[:, None, :, None] + 1.0)
    spread = lax.optimization_barrier(jnp.mean(plain * plain, axis=(1, 2, 3)))
    refs = (plain / jnp.sqrt(spread + 1e-06)[:, None, None, None]).reshape(CLASSES, K).astype(jnp.bfloat16)
    modulated = (particles.astype(jnp.float32).reshape(PARTICLES, 2, CYCLES, MFREQ) * ctf_rows[:, None, :, None]).reshape(PARTICLES, K).astype(jnp.bfloat16)
    widened = modulated.astype(jnp.float32)
    scale = 1.0 / math.sqrt(K)

    def score(best, rotation):
        turned = rotate_refs(refs, rotation, ROT).astype(jnp.float32)
        found = jnp.dot(widened, turned.T, preferred_element_type=jnp.float32) * scale
        return (jnp.maximum(best, found), None)
    start_best = jnp.full((PARTICLES, CLASSES), -jnp.inf, jnp.float32)
    best_scores, _ = lax.scan(score, start_best, jnp.arange(ROT, dtype=jnp.int32))
    return (refs, best_scores)
```

```python
import functools
import math

import jax
import jax.numpy as jnp
import numpy as np
from jax import lax
from jax.experimental import pallas as pl
from jax.experimental.pallas import tpu as pltpu
from jax.sharding import PartitionSpec as P

CYCLES = 64
MFREQ = 64
CLS = 6
BLOCKS = 8
ROWS = BLOCKS * CLS
FINE = 4
K = 2 * CYCLES * MFREQ
MESH = pl.DeviceIdType.MESH
F32 = jnp.float32
BF16 = jnp.bfloat16


def pieces(x):
    high = x.astype(BF16)
    rest = x - high.astype(F32)
    mid = rest.astype(BF16)
    low = (rest - mid.astype(F32)).astype(BF16)
    return high, mid, low


def exact_right(select, x):
    return sum(jnp.dot(select, part, preferred_element_type=F32) for part in pieces(x))


def exact_left(x, select):
    return sum(jnp.dot(part, select, preferred_element_type=F32) for part in pieces(x))


def iota(shape, dim):
    return lax.broadcasted_iota(jnp.int32, shape, dim)


def sixth(x):
    return lax.shift_right_logical(x * 10923, 16)


def ones_where(cond):
    return jnp.where(cond, 1.0, 0.0).astype(BF16)


def column_onehot(row, count):
    size = row.shape[1]
    wide = jnp.where(iota((count, size), 0) == row, 1.0, 0.0)
    return wide.T.astype(BF16)


def kernel(
    n_dom, n_rot,
    particles_ref, assign_ref, rot_ref, group_ref, table_ref, trig_ref,
    refs_ref, scores_ref,
    spec, sums, sums_in, plain_all, spread_mine, spread_in, normed, left, right,
    outgoing, incoming, norm_mine, norm_in,
    load_sem, a_send, a_recv, c_send, c_recv, s_send, s_recv, r_send, r_recv,
    e_send, e_recv, n_send, n_recv,
):
    me = lax.axis_index("dom")
    zed = lax.axis_index("rot")
    count = particles_ref.shape[0]
    total = trig_ref.shape[0] // 2
    share = count // n_rot
    coarse = total // FINE
    cyc = CYCLES // n_rot
    half = cyc * MFREQ
    lanes = half // 4
    tiles = ROWS // 8 * (lanes // 128)
    classes = CLS * n_dom
    groups = table_ref.shape[0]

    barrier = pltpu.get_barrier_semaphore()

    def dom_peer(step):
        return (lax.rem(me + step, n_dom), zed)

    def rot_peer(step):
        return (me, lax.rem(zed + step, n_rot))

    for step in range(1, n_dom):
        pl.semaphore_signal(barrier, inc=1, device_id=dom_peer(step), device_id_type=MESH)
    for step in range(1, n_rot):
        pl.semaphore_signal(barrier, inc=1, device_id=rot_peer(step), device_id_type=MESH)

    loads = []
    for part in range(2):
        start = pl.multiple_of(part * CYCLES * MFREQ + zed * half, 128)
        loads.append(
            pltpu.make_async_copy(
                particles_ref.at[:, pl.ds(start, half)], spec.at[part], load_sem.at[part]
            )
        )
        loads[-1].start()

    def widen(x):
        return x if lanes == 128 else jnp.concatenate([x] * (lanes // 128), axis=1)

    group_hot = column_onehot(group_ref[...], groups)
    rows = exact_right(group_hot, table_ref[...])
    spreader = ones_where(iota((CYCLES, half), 0) == zed * cyc + iota((CYCLES, half), 1) // MFREQ)
    factors = exact_left(rows, spreader)
    turn_hot = column_onehot(rot_ref[...], total)
    cosine = widen(exact_right(turn_hot, trig_ref[:total]))
    sine = widen(exact_right(turn_hot, trig_ref[total:]))

    labels = assign_ref[...]
    place = iota((n_dom * 8, count), 0)
    wanted = jnp.where((place & 7) < CLS, lax.shift_right_logical(place, 3) * CLS + (place & 7), -1)
    denom = exact_right(ones_where(wanted == labels), rows * rows)
    for owner in range(n_dom):
        sums[owner, tiles] = jnp.concatenate(
            [denom[owner * 8 : owner * 8 + 8], jnp.zeros((8, 128 - CYCLES), F32)], axis=1
        )

    place = iota((n_dom * ROWS, count), 0)
    six = sixth(place)
    block_of = six & (BLOCKS - 1)
    member = (lax.shift_right_logical(six, 3) * CLS + place - six * CLS) == labels

    for load in loads:
        load.wait()

    numer = jnp.zeros((n_dom * ROWS, lanes), F32)
    for block in range(BLOCKS):
        if block < 4:
            lane = slice(block * lanes, block * lanes + lanes)
            re = spec[0, :, lane].astype(F32)
            im = spec[1, :, lane].astype(F32)
            value = (re * cosine + im * sine) * factors[:, lane]
        else:
            lane = slice((block - 4) * lanes, (block - 4) * lanes + lanes)
            re = spec[0, :, lane].astype(F32)
            im = spec[1, :, lane].astype(F32)
            value = (im * cosine - re * sine) * factors[:, lane]
        chosen = ones_where(member & (block_of == block))
        stacked = jnp.concatenate([chosen] * 3, axis=1)
        numer += jnp.dot(
            stacked, jnp.concatenate(pieces(value), axis=0), preferred_element_type=F32
        )
    per_row = lanes // 128
    for owner in range(n_dom):
        for i in range(ROWS // 8):
            for j in range(per_row):
                first = owner * ROWS + i * 8
                sums[owner, i * per_row + j] = numer[first : first + 8, j * 128 : j * 128 + 128]

    pl.semaphore_wait(barrier, n_dom + n_rot - 2)

    a_copies = []
    for step in range(1, n_dom):
        a_copies.append(
            pltpu.make_async_remote_copy(
                src_ref=sums.at[lax.rem(me + step, n_dom)],
                dst_ref=sums_in.at[step - 1],
                send_sem=a_send.at[step - 1],
                recv_sem=a_recv.at[step - 1],
                device_id=dom_peer(step),
                device_id_type=MESH,
            )
        )
        a_copies[-1].start()

    for block in range(4):
        lane = slice(block * lanes, block * lanes + lanes)
        re = (spec[0, :, lane].astype(F32) * factors[:, lane]).astype(BF16).astype(F32)
        im = (spec[1, :, lane].astype(F32) * factors[:, lane]).astype(BF16).astype(F32)
        turned_re, turned_im = [], []
        for a in range(coarse):
            cos = widen(trig_ref[a * FINE : a * FINE + 1])
            sin = widen(trig_ref[total + a * FINE : total + a * FINE + 1])
            turned_re.append(re * cos + im * sin)
            turned_im.append(im * cos - re * sin)
        for part, turned in enumerate((turned_re, turned_im)):
            first = (part * 4 + block) * lanes
            for z in range(n_rot):
                left[z * 128 : z * 128 + 128, first : first + lanes] = jnp.concatenate(
                    [x[z * share : z * share + share] for x in turned], axis=0
                ).astype(BF16)

    for copy in a_copies:
        copy.wait_recv()

    whole = sums[me]
    for step in range(n_dom - 1):
        whole = whole + sums_in[step]
    numer = jnp.concatenate(
        [
            jnp.concatenate([whole[i * per_row + j] for j in range(per_row)], axis=1)
            for i in range(ROWS // 8)
        ],
        axis=0,
    )
    place = iota((ROWS, 8), 0)
    pick = ones_where(place - sixth(place) * CLS == iota((ROWS, 8), 1))
    denom = exact_right(pick, whole[tiles])
    cb = cyc // 4
    offset = iota((ROWS, 128), 1) - zed * cyc
    low = (sixth(iota((ROWS, 128), 0)) & 3) * cb
    denom = jnp.where((offset >= low) & (offset < low + cb), denom, 0.0)
    where_to = (iota((128, lanes), 0) & (cb - 1)) == iota((128, lanes), 1) // MFREQ
    denom = exact_left(denom, ones_where(where_to))
    plain = numer / (denom + 1.0)
    plain_all[me] = plain.astype(BF16)

    c_copies = []
    for step in range(1, n_dom):
        c_copies.append(
            pltpu.make_async_remote_copy(
                src_ref=plain_all.at[me],
                dst_ref=plain_all.at[me],
                send_sem=c_send.at[step - 1],
                recv_sem=c_recv.at[step - 1],
                device_id=dom_peer(step),
                device_id_type=MESH,
            )
        )
        c_copies[-1].start()

    squares = jnp.sum(plain * plain, axis=1, keepdims=True)
    place = iota((ROWS, ROWS), 0)
    other = iota((ROWS, ROWS), 1)
    same = ones_where(place - sixth(place) * CLS == other - sixth(other) * CLS)
    spread_mine[...] = exact_right(same, jnp.broadcast_to(squares, (ROWS, 128)))
    s_copies = []
    for step in range(1, n_rot):
        s_copies.append(
            pltpu.make_async_remote_copy(
                src_ref=spread_mine,
                dst_ref=spread_in.at[step - 1],
                send_sem=s_send.at[step - 1],
                recv_sem=s_recv.at[step - 1],
                device_id=rot_peer(step),
                device_id_type=MESH,
            )
        )
        s_copies[-1].start()
    for copy in s_copies:
        copy.wait_recv()
    spread = spread_mine[...]
    for step in range(n_rot - 1):
        spread = spread + spread_in[step]
    root = jnp.sqrt(spread / K + 1e-6)
    normed[zed] = (plain / widen(root)).astype(BF16)
    r_copies = []
    for step in range(1, n_rot):
        r_copies.append(
            pltpu.make_async_remote_copy(
                src_ref=normed.at[zed],
                dst_ref=normed.at[zed],
                send_sem=r_send.at[step - 1],
                recv_sem=r_recv.at[step - 1],
                device_id=rot_peer(step),
                device_id_type=MESH,
            )
        )
        r_copies[-1].start()

    for copy in c_copies:
        copy.wait_recv()

    gathered = plain_all[...].reshape(n_dom * ROWS, lanes)
    place = iota((classes, n_dom * ROWS), 0)
    owner = sixth(place)
    source = owner * ROWS + place - owner * CLS
    other = iota((classes, n_dom * ROWS), 1)
    blocks = [
        jnp.dot(
            ones_where(source + block * CLS == other), gathered, preferred_element_type=F32
        )
        for block in range(BLOCKS)
    ]
    for fine in range(FINE):
        cos = widen(trig_ref[fine : fine + 1])
        sin = widen(trig_ref[total + fine : total + fine + 1])
        for block in range(4):
            re, im = blocks[block], blocks[block + 4]
            at = slice(fine * classes, fine * classes + classes)
            right[at, block * lanes : block * lanes + lanes] = (re * cos - im * sin).astype(BF16)
            right[at, (block + 4) * lanes : (block + 4) * lanes + lanes] = (
                re * sin + im * cos
            ).astype(BF16)

    def partial(z):
        return lax.dot_general(
            right[...],
            left[pl.ds(pl.multiple_of(z * 128, 128), 128), :],
            (((1,), (1,)), ((), ())),
            preferred_element_type=F32,
        )

    e_copies = []
    for step in range(1, n_rot):
        outgoing[step - 1] = partial(lax.rem(zed + step, n_rot)).astype(BF16)
        e_copies.append(
            pltpu.make_async_remote_copy(
                src_ref=outgoing.at[step - 1],
                dst_ref=incoming.at[step - 1],
                send_sem=e_send.at[step - 1],
                recv_sem=e_recv.at[step - 1],
                device_id=rot_peer(step),
                device_id_type=MESH,
            )
        )
        e_copies[-1].start()
    found = partial(zed)

    squares = jnp.zeros((classes, lanes), F32)
    for block in blocks:
        squares = squares + block * block
    squares = jnp.broadcast_to(jnp.sum(squares, axis=1, keepdims=True), (classes, 128))
    norm_mine[...] = squares.T[:8]
    n_copies = []
    for step in range(1, n_rot):
        n_copies.append(
            pltpu.make_async_remote_copy(
                src_ref=norm_mine,
                dst_ref=norm_in.at[step - 1],
                send_sem=n_send.at[step - 1],
                recv_sem=n_recv.at[step - 1],
                device_id=rot_peer(step),
                device_id_type=MESH,
            )
        )
        n_copies[-1].start()

    for copy in r_copies:
        copy.wait_recv()
    for z in range(n_rot):
        mine = normed[z].astype(F32)
        for block in range(BLOCKS):
            first = (block // 4) * CYCLES * MFREQ + z * half + (block % 4) * lanes
            refs_ref[:, first : first + lanes] = mine[block * CLS : block * CLS + CLS].astype(BF16)

    for copy in n_copies:
        copy.wait_recv()
    spread = norm_mine[...]
    for step in range(n_rot - 1):
        spread = spread + norm_in[step]
    scale = (1.0 / math.sqrt(K)) / jnp.sqrt(spread / K + 1e-6)

    for step, copy in enumerate(e_copies):
        copy.wait_recv()
        found = found + incoming[step].astype(F32)
    best = found[:classes]
    for fine in range(1, FINE):
        best = jnp.maximum(best, found[fine * classes : fine * classes + classes])
    best = best.T
    top = best[:share]
    for a in range(1, coarse):
        top = jnp.maximum(top, best[a * share : a * share + share])
    scores_ref[...] = top * scale[:1]

    for copy in a_copies + c_copies + s_copies + r_copies + e_copies + n_copies:
        copy.wait_send()


def trig_table(total):
    freqs = np.arange(128) % MFREQ
    phase = (np.arange(total)[:, None] * freqs[None, :]) % total * (2.0 * math.pi / total)
    return np.concatenate([np.cos(phase), np.sin(phase)]).astype(np.float32)


def local(n_dom, n_rot, particles, assign, rot_index, group, ctf_table):
    count = particles.shape[0]
    total = 8 * n_rot
    share = count // n_rot
    lanes = CYCLES // n_rot * MFREQ // 4
    half = 4 * lanes
    tiles = ROWS // 8 * (lanes // 128)
    classes = CLS * n_dom
    vmem = pl.BlockSpec(memory_space=pltpu.VMEM)
    dma = pltpu.SemaphoreType.DMA
    dom, rot = dma((n_dom - 1,)), dma((n_rot - 1,))
    return pl.pallas_call(
        functools.partial(kernel, n_dom, n_rot),
        out_shape=(
            jax.ShapeDtypeStruct((CLS, K), BF16),
            jax.ShapeDtypeStruct((share, classes), F32),
        ),
        in_specs=[pl.BlockSpec(memory_space=pl.ANY)] + [vmem] * 5,
        out_specs=(vmem, vmem),
        scratch_shapes=[
            pltpu.VMEM((2, count, half), BF16),
            pltpu.VMEM((n_dom, tiles + 1, 8, 128), F32),
            pltpu.VMEM((n_dom - 1, tiles + 1, 8, 128), F32),
            pltpu.VMEM((n_dom, ROWS, lanes), BF16),
            pltpu.VMEM((ROWS, 128), F32),
            pltpu.VMEM((n_rot - 1, ROWS, 128), F32),
            pltpu.VMEM((n_rot, ROWS, lanes), BF16),
            pltpu.VMEM((n_rot * 128, 8 * lanes), BF16),
            pltpu.VMEM((FINE * classes, 8 * lanes), BF16),
            pltpu.VMEM((n_rot - 1, FINE * classes, 128), BF16),
            pltpu.VMEM((n_rot - 1, FINE * classes, 128), BF16),
            pltpu.VMEM((8, classes), F32),
            pltpu.VMEM((n_rot - 1, 8, classes), F32),
            dma((2,)),
            dom, dom, dom, dom, rot, rot, rot, rot, rot, rot, rot, rot,
        ],
        compiler_params=pltpu.CompilerParams(
            collective_id=0, has_side_effects=True, vmem_limit_bytes=48 * 1024 * 1024
        ),
    )(
        particles,
        assign.reshape(1, count),
        rot_index.reshape(1, count),
        group.reshape(1, count),
        ctf_table,
        jnp.asarray(trig_table(total)),
    )


def solution(mesh):
    sizes = dict(mesh.shape)
    in_specs = (P("dom", None), P("dom"), P("dom"), P("dom"), P())
    out_specs = (P("dom", None), P(("dom", "rot"), None))
    return jax.shard_map(
        functools.partial(local, sizes["dom"], sizes["rot"]),
        mesh=mesh, in_specs=in_specs, out_specs=out_specs, check_vma=False,
    )
```

```python
import functools
import math

import jax
import jax.numpy as jnp
import numpy as np
from jax import lax
from jax.experimental import pallas as pl
from jax.experimental.pallas import tpu as pltpu
from jax.sharding import PartitionSpec as P

CYCLES = 64
MFREQ = 64
CLS = 6
BLOCKS = 8
ROWS = BLOCKS * CLS
FINE = 4
K = 2 * CYCLES * MFREQ
MESH = pl.DeviceIdType.MESH
F32 = jnp.float32
BF16 = jnp.bfloat16


def pieces(x):
    high = x.astype(BF16)
    rest = x - high.astype(F32)
    mid = rest.astype(BF16)
    low = (rest - mid.astype(F32)).astype(BF16)
    return high, mid, low


def stacked(x):
    return jnp.concatenate(pieces(x), axis=0)


def iota(shape, dim):
    return lax.broadcasted_iota(jnp.int32, shape, dim)


def ones_where(cond):
    return jnp.where(cond, 1.0, 0.0).astype(BF16)


def dot(x, y):
    return jnp.dot(x, y, preferred_element_type=F32)


def column_onehot(row, count):
    shape = (3 * count, row.shape[1])
    return jnp.where((iota(shape, 0) & (count - 1)) == row, 1.0, 0.0).T.astype(BF16)


def each_row(tile):
    return jnp.concatenate([jnp.broadcast_to(tile[c : c + 1], (8, 128)) for c in range(CLS)], axis=0)


def kernel(
    n_dom, n_rot,
    particles_hbm, assign_hbm, rot_hbm, group_hbm, table_hbm, trig_hbm,
    refs_ref, scores_ref,
    spec, assign_ref, rot_ref, group_ref, table_ref, trig_ref,
    sums, sums_in, plain_all, wide, spread_mine, spread_in, normed, left, right,
    outgoing, incoming, norm_mine, norm_in,
    load_sem, a_send, a_recv, c_send, c_recv, s_send, s_recv, r_send, r_recv,
    e_send, e_recv, n_send, n_recv,
):
    me = lax.axis_index("dom")
    zed = lax.axis_index("rot")
    count = spec.shape[1]
    total = trig_ref.shape[0]
    share = count // n_rot
    coarse = total // FINE
    cyc = CYCLES // n_rot
    half = cyc * MFREQ
    lanes = half // 4
    per_row = lanes // 128
    classes = CLS * n_dom
    groups = table_ref.shape[0]

    barrier = pltpu.get_barrier_semaphore()

    def dom_peer(step):
        return (lax.rem(me + step, n_dom), zed)

    def rot_peer(step):
        return (me, lax.rem(zed + step, n_rot))

    for step in range(1, n_dom):
        pl.semaphore_signal(barrier, inc=1, device_id=dom_peer(step), device_id_type=MESH)
    for step in range(1, n_rot):
        pl.semaphore_signal(barrier, inc=1, device_id=rot_peer(step), device_id_type=MESH)

    pairs = [(group_hbm, group_ref), (table_hbm, table_ref), (rot_hbm, rot_ref)]
    pairs += [(trig_hbm, trig_ref), (assign_hbm, assign_ref)]
    for part in range(2):
        start = pl.multiple_of(part * CYCLES * MFREQ + zed * half, 128)
        pairs.append((particles_hbm.at[:, pl.ds(start, half)], spec.at[part]))
    loads = [pltpu.make_async_copy(x, y, load_sem.at[i]) for i, (x, y) in enumerate(pairs)]
    for load in loads:
        load.start()

    def widen(x):
        return x if per_row == 1 else jnp.concatenate([x] * per_row, axis=1)

    def side_by_side(take):
        tiles = [take(i) for i in range(per_row)]
        return tiles[0] if per_row == 1 else jnp.concatenate(tiles, axis=1)

    shape = (3 * CYCLES, half)
    spreader = ones_where((iota(shape, 0) & (CYCLES - 1)) == zed * cyc + iota(shape, 1) // MFREQ)
    loads[0].wait()
    loads[1].wait()
    rows = dot(column_onehot(group_ref[...], groups), stacked(table_ref[...]))
    factors = dot(jnp.concatenate(pieces(rows), axis=1), spreader)
    loads[2].wait()
    loads[3].wait()
    turns = dot(column_onehot(rot_ref[...], total), stacked(trig_ref[...]))
    cosine, sine = widen(turns[:, :128]), widen(turns[:, 128:])

    loads[4].wait()
    labels = jnp.concatenate([assign_ref[...]] * 3, axis=1)
    place = iota((classes, 3 * count), 0)
    member = ones_where((place & (n_dom - 1)) * CLS + place // n_dom == labels)
    denom = dot(member, stacked(rows * rows))
    denom = jnp.concatenate([denom, jnp.zeros((classes, 128 - CYCLES), F32)], axis=1)
    for c in range(CLS):
        at = pl.ds(ROWS + c, n_dom, stride=ROWS + 8)
        sums[0, at, :] = denom[c * n_dom : c * n_dom + n_dom]

    loads[5].wait()
    loads[6].wait()
    for block in range(4):
        lane = slice(block * lanes, block * lanes + lanes)
        re = spec[0, :, lane].astype(F32)
        im = spec[1, :, lane].astype(F32)
        both = (re * cosine + im * sine, im * cosine - re * sine)
        for part, value in enumerate(both):
            numer = dot(member, stacked(value * factors[:, lane]))
            for c in range(CLS):
                at = pl.ds(c * 8 + part * 4 + block, n_dom, stride=ROWS + 8)
                for i in range(per_row):
                    sums[i, at, :] = numer[c * n_dom : c * n_dom + n_dom, i * 128 : i * 128 + 128]

    pl.semaphore_wait(barrier, n_dom + n_rot - 2)

    def owned(owner):
        return sums.at[:, pl.ds(pl.multiple_of(owner * (ROWS + 8), 8), ROWS + 8), :]

    a_copies = []
    for step in range(1, n_dom):
        a_copies.append(
            pltpu.make_async_remote_copy(
                src_ref=owned(lax.rem(me + step, n_dom)),
                dst_ref=sums_in.at[step - 1],
                send_sem=a_send.at[step - 1],
                recv_sem=a_recv.at[step - 1],
                device_id=dom_peer(step),
                device_id_type=MESH,
            )
        )
        a_copies[-1].start()

    for block in range(4):
        lane = slice(block * lanes, block * lanes + lanes)
        re = (spec[0, :, lane].astype(F32) * factors[:, lane]).astype(BF16).astype(F32)
        im = (spec[1, :, lane].astype(F32) * factors[:, lane]).astype(BF16).astype(F32)
        turned_re, turned_im = [], []
        for a in range(coarse):
            cos = widen(trig_ref[a * FINE : a * FINE + 1, :128])
            sin = widen(trig_ref[a * FINE : a * FINE + 1, 128:])
            turned_re.append(re * cos + im * sin)
            turned_im.append(im * cos - re * sin)
        for part, turned in enumerate((turned_re, turned_im)):
            first = (part * 4 + block) * lanes
            for z in range(n_rot):
                left[z * 128 : z * 128 + 128, first : first + lanes] = jnp.concatenate(
                    [x[z * share : z * share + share] for x in turned], axis=0
                ).astype(BF16)

    cb = cyc // 4
    offset = iota((ROWS, 128), 1) - zed * cyc
    low = (iota((ROWS, 128), 0) & 3) * cb
    shape = (3 * 128, lanes)
    spreader = ones_where((iota(shape, 0) & (cb - 1)) == iota(shape, 1) // MFREQ)

    for copy in a_copies:
        copy.wait_recv()

    whole = owned(me)[...]
    for step in range(n_dom - 1):
        whole = whole + sums_in[step]
    numer = side_by_side(lambda i: whole[i, :ROWS])
    denom = jnp.where((offset >= low) & (offset < low + cb), each_row(whole[0, ROWS:]), 0.0)
    denom = dot(jnp.concatenate(pieces(denom), axis=1), spreader)
    plain = numer / (denom + 1.0)
    plain_all[me] = plain.astype(BF16)

    c_copies = []
    for step in range(1, n_dom):
        c_copies.append(
            pltpu.make_async_remote_copy(
                src_ref=plain_all.at[me],
                dst_ref=plain_all.at[me],
                send_sem=c_send.at[step - 1],
                recv_sem=c_recv.at[step - 1],
                device_id=dom_peer(step),
                device_id_type=MESH,
            )
        )
        c_copies[-1].start()

    squares = jnp.sum((plain * plain).reshape(CLS, 8, lanes), axis=1)
    squares = jnp.broadcast_to(jnp.sum(squares, axis=1, keepdims=True), (CLS, 128))
    spread_mine[...] = jnp.concatenate([squares, jnp.zeros((8 - CLS, 128), F32)], axis=0)
    s_copies = []
    for step in range(1, n_rot):
        s_copies.append(
            pltpu.make_async_remote_copy(
                src_ref=spread_mine,
                dst_ref=spread_in.at[step - 1],
                send_sem=s_send.at[step - 1],
                recv_sem=s_recv.at[step - 1],
                device_id=rot_peer(step),
                device_id_type=MESH,
            )
        )
        s_copies[-1].start()
    for copy in s_copies:
        copy.wait_recv()
    spread = spread_mine[...]
    for step in range(n_rot - 1):
        spread = spread + spread_in[step]
    root = each_row(jnp.sqrt(spread / K + 1e-6))
    normed[zed] = (plain / widen(root)).astype(BF16)
    r_copies = []
    for step in range(1, n_rot):
        r_copies.append(
            pltpu.make_async_remote_copy(
                src_ref=normed.at[zed],
                dst_ref=normed.at[zed],
                send_sem=r_send.at[step - 1],
                recv_sem=r_recv.at[step - 1],
                device_id=rot_peer(step),
                device_id_type=MESH,
            )
        )
        r_copies[-1].start()

    for copy in c_copies:
        copy.wait_recv()

    for i in range(per_row):
        wide[i] = plain_all[:, :, i * 128 : i * 128 + 128].astype(F32).reshape(classes * 8, 128)
    blocks = [
        side_by_side(lambda i: wide[i, pl.ds(block, classes, stride=8), :])
        for block in range(BLOCKS)
    ]
    for fine in range(FINE):
        cos = widen(trig_ref[fine : fine + 1, :128])
        sin = widen(trig_ref[fine : fine + 1, 128:])
        for block in range(4):
            re, im = blocks[block], blocks[block + 4]
            at = slice(fine * classes, fine * classes + classes)
            right[at, block * lanes : block * lanes + lanes] = (re * cos - im * sin).astype(BF16)
            right[at, (block + 4) * lanes : (block + 4) * lanes + lanes] = (
                re * sin + im * cos
            ).astype(BF16)

    def partial(z):
        return lax.dot_general(
            right[...],
            left[pl.ds(pl.multiple_of(z * 128, 128), 128), :],
            (((1,), (1,)), ((), ())),
            preferred_element_type=F32,
        )

    e_copies = []
    for step in range(1, n_rot):
        outgoing[step - 1] = partial(lax.rem(zed + step, n_rot)).astype(BF16)
        e_copies.append(
            pltpu.make_async_remote_copy(
                src_ref=outgoing.at[step - 1],
                dst_ref=incoming.at[step - 1],
                send_sem=e_send.at[step - 1],
                recv_sem=e_recv.at[step - 1],
                device_id=rot_peer(step),
                device_id_type=MESH,
            )
        )
        e_copies[-1].start()

    squares = jnp.zeros((classes, lanes), F32)
    for block in range(BLOCKS):
        x = side_by_side(lambda i: wide[i, pl.ds(block, classes, stride=8), :])
        squares = squares + x * x
    squares = jnp.broadcast_to(jnp.sum(squares, axis=1, keepdims=True), (classes, 128))
    norm_mine[...] = squares.T[:8]
    n_copies = []
    for step in range(1, n_rot):
        n_copies.append(
            pltpu.make_async_remote_copy(
                src_ref=norm_mine,
                dst_ref=norm_in.at[step - 1],
                send_sem=n_send.at[step - 1],
                recv_sem=n_recv.at[step - 1],
                device_id=rot_peer(step),
                device_id_type=MESH,
            )
        )
        n_copies[-1].start()
    found = partial(zed)

    for copy in r_copies:
        copy.wait_recv()
    for z in range(n_rot):
        for i in range(per_row):
            wide[i, :ROWS] = normed[z, :, i * 128 : i * 128 + 128].astype(F32)
            for block in range(BLOCKS):
                first = (block // 4) * CYCLES * MFREQ + z * half + (block % 4) * lanes + i * 128
                refs_ref[:, first : first + 128] = wide[i, pl.ds(block, CLS, stride=8), :].astype(
                    BF16
                )

    for copy in n_copies:
        copy.wait_recv()
    spread = norm_mine[...]
    for step in range(n_rot - 1):
        spread = spread + norm_in[step]
    scale = (1.0 / math.sqrt(K)) / jnp.sqrt(spread / K + 1e-6)

    for step, copy in enumerate(e_copies):
        copy.wait_recv()
        found = found + incoming[step].astype(F32)
    best = found[:classes]
    for fine in range(1, FINE):
        best = jnp.maximum(best, found[fine * classes : fine * classes + classes])
    best = best.T
    top = best[:share]
    for a in range(1, coarse):
        top = jnp.maximum(top, best[a * share : a * share + share])
    scores_ref[...] = top * scale[:1]

    for copy in a_copies + c_copies + s_copies + r_copies + e_copies + n_copies:
        copy.wait_send()


def trig_table(total):
    freqs = np.arange(128) % MFREQ
    phase = (np.arange(total)[:, None] * freqs[None, :]) % total * (2.0 * math.pi / total)
    return np.concatenate([np.cos(phase), np.sin(phase)], axis=1).astype(np.float32)


def local(n_dom, n_rot, particles, assign, rot_index, group, ctf_table):
    count = particles.shape[0]
    total = 8 * n_rot
    share = count // n_rot
    lanes = CYCLES // n_rot * MFREQ // 4
    half = 4 * lanes
    per_row = lanes // 128
    classes = CLS * n_dom
    vmem = pl.BlockSpec(memory_space=pltpu.VMEM)
    dma = pltpu.SemaphoreType.DMA
    dom, rot = dma((n_dom - 1,)), dma((n_rot - 1,))
    return pl.pallas_call(
        functools.partial(kernel, n_dom, n_rot),
        out_shape=(
            jax.ShapeDtypeStruct((CLS, K), BF16),
            jax.ShapeDtypeStruct((share, classes), F32),
        ),
        in_specs=[pl.BlockSpec(memory_space=pltpu.HBM)] * 6,
        out_specs=(vmem, vmem),
        scratch_shapes=[
            pltpu.VMEM((2, count, half), BF16),
            pltpu.VMEM((1, count), jnp.int32),
            pltpu.VMEM((1, count), jnp.int32),
            pltpu.VMEM((1, count), jnp.int32),
            pltpu.VMEM(ctf_table.shape, F32),
            pltpu.VMEM((total, 256), F32),
            pltpu.VMEM((per_row, n_dom * (ROWS + 8), 128), F32),
            pltpu.VMEM((n_dom - 1, per_row, ROWS + 8, 128), F32),
            pltpu.VMEM((n_dom, ROWS, lanes), BF16),
            pltpu.VMEM((per_row, n_dom * ROWS, 128), F32),
            pltpu.VMEM((8, 128), F32),
            pltpu.VMEM((n_rot - 1, 8, 128), F32),
            pltpu.VMEM((n_rot, ROWS, lanes), BF16),
            pltpu.VMEM((n_rot * 128, 8 * lanes), BF16),
            pltpu.VMEM((FINE * classes, 8 * lanes), BF16),
            pltpu.VMEM((n_rot - 1, FINE * classes, 128), BF16),
            pltpu.VMEM((n_rot - 1, FINE * classes, 128), BF16),
            pltpu.VMEM((8, classes), F32),
            pltpu.VMEM((n_rot - 1, 8, classes), F32),
            dma((7,)),
            dom, dom, dom, dom, rot, rot, rot, rot, rot, rot, rot, rot,
        ],
        compiler_params=pltpu.CompilerParams(
            collective_id=0, has_side_effects=True, vmem_limit_bytes=48 * 1024 * 1024
        ),
    )(
        *(
            pltpu.with_memory_space_constraint(x, pltpu.HBM)
            for x in (
                particles,
                assign.reshape(1, count),
                rot_index.reshape(1, count),
                group.reshape(1, count),
                ctf_table,
                jnp.asarray(trig_table(total)),
            )
        )
    )


def solution(mesh):
    sizes = dict(mesh.shape)
    in_specs = (P("dom", None), P("dom"), P("dom"), P("dom"), P())
    out_specs = (P("dom", None), P(("dom", "rot"), None))
    return jax.shard_map(
        functools.partial(local, sizes["dom"], sizes["rot"]),
        mesh=mesh, in_specs=in_specs, out_specs=out_specs, check_vma=False,
    )
```

```python
import functools
import math

import jax
import jax.numpy as jnp
import numpy as np
from jax import lax
from jax.experimental import pallas as pl
from jax.experimental.pallas import tpu as pltpu
from jax.sharding import PartitionSpec as P

CYCLES = 64
MFREQ = 64
CLS = 6
BLOCKS = 8
ROWS = BLOCKS * CLS
FINE = 4
K = 2 * CYCLES * MFREQ
MESH = pl.DeviceIdType.MESH
F32 = jnp.float32
BF16 = jnp.bfloat16


def pieces(x):
    high = x.astype(BF16)
    rest = x - high.astype(F32)
    mid = rest.astype(BF16)
    low = (rest - mid.astype(F32)).astype(BF16)
    return high, mid, low


def stacked(x):
    return jnp.concatenate(pieces(x), axis=0)


def iota(shape, dim):
    return lax.broadcasted_iota(jnp.int32, shape, dim)


def ones_where(cond):
    return jnp.where(cond, 1.0, 0.0).astype(BF16)


def dot(x, y):
    return jnp.dot(x, y, preferred_element_type=F32)


def column_onehot(row, count):
    shape = (3 * count, row.shape[1])
    return jnp.where((iota(shape, 0) & (count - 1)) == row, 1.0, 0.0).T.astype(BF16)


def each_row(tile):
    return jnp.concatenate([jnp.broadcast_to(tile[c : c + 1], (8, 128)) for c in range(CLS)], axis=0)


def kernel(
    n_dom, n_rot,
    particles_hbm, assign_hbm, rot_hbm, group_hbm, table_hbm, trig_hbm,
    refs_ref, scores_ref,
    spec, assign_ref, rot_ref, group_ref, table_ref, trig_ref,
    sums, sums_in, plain_all, wide, spread_mine, spread_in, normed, left, right,
    earlier, outgoing, incoming, norm_mine, norm_in,
    load_sem, a_send, a_recv, c_send, c_recv, s_send, s_recv, r_send, r_recv,
    e_send, e_recv, n_send, n_recv,
):
    me = lax.axis_index("dom")
    zed = lax.axis_index("rot")
    count = spec.shape[1]
    total = trig_ref.shape[0]
    share = count // n_rot
    coarse = total // FINE
    cyc = CYCLES // n_rot
    half = cyc * MFREQ
    lanes = half // 4
    per_row = lanes // 128
    classes = CLS * n_dom
    groups = table_ref.shape[0]

    barrier = pltpu.get_barrier_semaphore()

    def dom_peer(step):
        return (lax.rem(me + step, n_dom), zed)

    def rot_peer(step):
        return (me, lax.rem(zed + step, n_rot))

    for step in range(1, n_dom):
        pl.semaphore_signal(barrier, inc=1, device_id=dom_peer(step), device_id_type=MESH)
    for step in range(1, n_rot):
        pl.semaphore_signal(barrier, inc=1, device_id=rot_peer(step), device_id_type=MESH)

    pairs = [(group_hbm, group_ref), (table_hbm, table_ref), (rot_hbm, rot_ref)]
    pairs += [(trig_hbm, trig_ref), (assign_hbm, assign_ref)]
    for part in range(2):
        start = pl.multiple_of(part * CYCLES * MFREQ + zed * half, 128)
        pairs.append((particles_hbm.at[:, pl.ds(start, half)], spec.at[part]))
    loads = [pltpu.make_async_copy(x, y, load_sem.at[i]) for i, (x, y) in enumerate(pairs)]
    for load in loads:
        load.start()

    shape = (3 * CYCLES, half)
    spreader = ones_where((iota(shape, 0) & (CYCLES - 1)) == zed * cyc + iota(shape, 1) // MFREQ)
    loads[0].wait()
    loads[1].wait()
    rows = dot(column_onehot(group_ref[...], groups), stacked(table_ref[...]))
    factors = dot(jnp.concatenate(pieces(rows), axis=1), spreader)
    loads[2].wait()
    loads[3].wait()
    turns = dot(column_onehot(rot_ref[...], total), stacked(trig_ref[...]))
    cosine, sine = turns[:, :128], turns[:, 128:]

    loads[4].wait()
    labels = jnp.concatenate([assign_ref[...]] * 3, axis=1)
    place = iota((classes, 3 * count), 0)
    member = ones_where((place & (n_dom - 1)) * CLS + place // n_dom == labels)
    denom = dot(member, stacked(rows * rows))
    denom = jnp.concatenate([denom, jnp.zeros((classes, 128 - CYCLES), F32)], axis=1)
    for c in range(CLS):
        at = pl.ds(ROWS + c, n_dom, stride=ROWS + 8)
        sums[0, at, :] = denom[c * n_dom : c * n_dom + n_dom]

    def message(part, owner):
        first = pl.multiple_of(owner * (ROWS + 8), 8)
        return sums.at[part, pl.ds(first, ROWS + 8 if part == 0 else ROWS), :]

    def landing(part, step):
        return sums_in.at[step - 1, part, pl.ds(0, ROWS + 8 if part == 0 else ROWS), :]

    def lane_tile(block, part):
        first = block * lanes + part * 128
        return slice(first, first + 128)

    loads[5].wait()
    loads[6].wait()
    a_copies = []
    for part in range(per_row):
        for block in range(4):
            lane = lane_tile(block, part)
            re = spec[0, :, lane].astype(F32)
            im = spec[1, :, lane].astype(F32)
            both = [re * cosine + im * sine, im * cosine - re * sine]
            value = jnp.concatenate([x * factors[:, lane] for x in both], axis=1)
            numer = dot(member, stacked(value))
            for c in range(CLS):
                for i in range(2):
                    at = pl.ds(c * 8 + i * 4 + block, n_dom, stride=ROWS + 8)
                    sums[part, at, :] = numer[
                        c * n_dom : c * n_dom + n_dom, i * 128 : i * 128 + 128
                    ]
        if part == 0:
            pl.semaphore_wait(barrier, n_dom + n_rot - 2)
        group_copies = []
        for step in range(1, n_dom):
            group_copies.append(
                pltpu.make_async_remote_copy(
                    src_ref=message(part, lax.rem(me + step, n_dom)),
                    dst_ref=landing(part, step),
                    send_sem=a_send.at[part, step - 1],
                    recv_sem=a_recv.at[part, step - 1],
                    device_id=dom_peer(step),
                    device_id_type=MESH,
                )
            )
            group_copies[-1].start()
        a_copies.append(group_copies)

    for part in range(per_row):
        for block in range(4):
            lane = lane_tile(block, part)
            re = (spec[0, :, lane].astype(F32) * factors[:, lane]).astype(BF16).astype(F32)
            im = (spec[1, :, lane].astype(F32) * factors[:, lane]).astype(BF16).astype(F32)
            turned_re, turned_im = [], []
            for a in range(coarse):
                cos = trig_ref[a * FINE : a * FINE + 1, :128]
                sin = trig_ref[a * FINE : a * FINE + 1, 128:]
                turned_re.append(re * cos + im * sin)
                turned_im.append(im * cos - re * sin)
            for i, turned in enumerate((turned_re, turned_im)):
                first = (i * 4 + block) * 128
                for z in range(n_rot):
                    left[part, z * 128 : z * 128 + 128, first : first + 128] = jnp.concatenate(
                        [x[z * share : z * share + share] for x in turned], axis=0
                    ).astype(BF16)

    cb = cyc // 4
    offset = iota((ROWS, 128), 1) - zed * cyc
    low = (iota((ROWS, 128), 0) & 3) * cb
    shape = (3 * 128, lanes)
    spreader = ones_where((iota(shape, 0) & (cb - 1)) == iota(shape, 1) // MFREQ)

    c_copies = []
    plain = []
    for part in range(per_row):
        for copy in a_copies[part]:
            copy.wait_recv()
        whole = message(part, me)[...]
        for step in range(1, n_dom):
            whole = whole + landing(part, step)[...]
        if part == 0:
            denom = jnp.where(
                (offset >= low) & (offset < low + cb), each_row(whole[ROWS:]), 0.0
            )
            denom = dot(jnp.concatenate(pieces(denom), axis=1), spreader) + 1.0
        plain.append(whole[:ROWS] / denom[:, part * 128 : part * 128 + 128])
        plain_all[part, me] = plain[-1].astype(BF16)
        group_copies = []
        for step in range(1, n_dom):
            group_copies.append(
                pltpu.make_async_remote_copy(
                    src_ref=plain_all.at[part, me],
                    dst_ref=plain_all.at[part, me],
                    send_sem=c_send.at[part, step - 1],
                    recv_sem=c_recv.at[part, step - 1],
                    device_id=dom_peer(step),
                    device_id_type=MESH,
                )
            )
            group_copies[-1].start()
        c_copies.append(group_copies)

    squares = sum(jnp.sum((x * x).reshape(CLS, 8, 128), axis=1) for x in plain)
    squares = jnp.broadcast_to(jnp.sum(squares, axis=1, keepdims=True), (CLS, 128))
    spread_mine[...] = jnp.concatenate([squares, jnp.zeros((8 - CLS, 128), F32)], axis=0)
    s_copies = []
    for step in range(1, n_rot):
        s_copies.append(
            pltpu.make_async_remote_copy(
                src_ref=spread_mine,
                dst_ref=spread_in.at[step - 1],
                send_sem=s_send.at[step - 1],
                recv_sem=s_recv.at[step - 1],
                device_id=rot_peer(step),
                device_id_type=MESH,
            )
        )
        s_copies[-1].start()

    def turn_references(part):
        for copy in c_copies[part]:
            copy.wait_recv()
        wide[part] = plain_all[part].astype(F32).reshape(classes * 8, 128)
        blocks = [wide[part, pl.ds(block, classes, stride=8), :] for block in range(BLOCKS)]
        for fine in range(FINE):
            cos = trig_ref[fine : fine + 1, :128]
            sin = trig_ref[fine : fine + 1, 128:]
            at = slice(fine * classes, fine * classes + classes)
            for block in range(4):
                re, im = blocks[block], blocks[block + 4]
                lane = slice(block * 128, block * 128 + 128)
                right[part, at, lane] = (re * cos - im * sin).astype(BF16)
                lane = slice(block * 128 + 512, block * 128 + 640)
                right[part, at, lane] = (re * sin + im * cos).astype(BF16)

    def product(part, rows):
        return lax.dot_general(
            right[part], rows, (((1,), (1,)), ((), ())), preferred_element_type=F32
        )

    for part in range(per_row - 1):
        turn_references(part)
        found = product(part, left[part])
        for z in range(n_rot):
            first = found[:, z * 128 : z * 128 + 128]
            earlier[z] = first if part == 0 else earlier[z] + first

    for copy in s_copies:
        copy.wait_recv()
    spread = spread_mine[...]
    for step in range(n_rot - 1):
        spread = spread + spread_in[step]
    root = each_row(jnp.sqrt(spread / K + 1e-6))
    for part in range(per_row):
        normed[zed, part] = (plain[part] / root).astype(BF16)
    r_copies = []
    for step in range(1, n_rot):
        r_copies.append(
            pltpu.make_async_remote_copy(
                src_ref=normed.at[zed],
                dst_ref=normed.at[zed],
                send_sem=r_send.at[step - 1],
                recv_sem=r_recv.at[step - 1],
                device_id=rot_peer(step),
                device_id_type=MESH,
            )
        )
        r_copies[-1].start()

    last = per_row - 1
    turn_references(last)

    def partial(z):
        rows = left[last, pl.ds(pl.multiple_of(z * 128, 128), 128), :]
        return product(last, rows) + earlier[z] if last else product(last, rows)

    steps = [n_rot // 2]
    for step in range(n_rot // 2 - 1, 0, -1):
        steps += [lax.select(zed % 2 == 0, n_rot - step, step)]
        steps += [lax.select(zed % 2 == 0, step, n_rot - step)]
    e_copies = []
    for i, step in enumerate(steps):
        outgoing[i] = partial(lax.rem(zed + step, n_rot)).astype(BF16)
        e_copies.append(
            pltpu.make_async_remote_copy(
                src_ref=outgoing.at[i],
                dst_ref=incoming.at[i],
                send_sem=e_send.at[i],
                recv_sem=e_recv.at[i],
                device_id=rot_peer(step),
                device_id_type=MESH,
            )
        )
        e_copies[-1].start()

    squares = jnp.zeros((classes, 128), F32)
    for part in range(per_row):
        for block in range(BLOCKS):
            x = wide[part, pl.ds(block, classes, stride=8), :]
            squares = squares + x * x
    squares = jnp.broadcast_to(jnp.sum(squares, axis=1, keepdims=True), (classes, 128))
    norm_mine[...] = squares.T[:8]
    n_copies = []
    for step in range(1, n_rot):
        n_copies.append(
            pltpu.make_async_remote_copy(
                src_ref=norm_mine,
                dst_ref=norm_in.at[step - 1],
                send_sem=n_send.at[step - 1],
                recv_sem=n_recv.at[step - 1],
                device_id=rot_peer(step),
                device_id_type=MESH,
            )
        )
        n_copies[-1].start()
    found = partial(zed)

    for copy in r_copies:
        copy.wait_recv()
    for z in range(n_rot):
        for part in range(per_row):
            wide[part, :ROWS] = normed[z, part].astype(F32)
            for block in range(BLOCKS):
                first = (block // 4) * CYCLES * MFREQ + z * half
                first += (block % 4) * lanes + part * 128
                values = wide[part, pl.ds(block, CLS, stride=8), :]
                refs_ref[:, first : first + 128] = values.astype(BF16)

    for copy in n_copies:
        copy.wait_recv()
    spread = norm_mine[...]
    for step in range(n_rot - 1):
        spread = spread + norm_in[step]
    scale = (1.0 / math.sqrt(K)) / jnp.sqrt(spread / K + 1e-6)

    for i, copy in enumerate(e_copies):
        copy.wait_recv()
        found = found + incoming[i].astype(F32)
    best = found[:classes]
    for fine in range(1, FINE):
        best = jnp.maximum(best, found[fine * classes : fine * classes + classes])
    best = best.T
    top = best[:share]
    for a in range(1, coarse):
        top = jnp.maximum(top, best[a * share : a * share + share])
    scores_ref[...] = top * scale[:1]

    for copy in sum(a_copies + c_copies, []) + s_copies + r_copies + e_copies + n_copies:
        copy.wait_send()


def write_out(refs, scores, refs_out, scores_out, sem):
    copies = [
        pltpu.make_async_copy(refs, refs_out, sem.at[0]),
        pltpu.make_async_copy(scores, scores_out, sem.at[1]),
    ]
    for copy in copies:
        copy.start()
    for copy in copies:
        copy.wait()


def trig_table(total):
    freqs = np.arange(128) % MFREQ
    phase = (np.arange(total)[:, None] * freqs[None, :]) % total * (2.0 * math.pi / total)
    return np.concatenate([np.cos(phase), np.sin(phase)], axis=1).astype(np.float32)


def local(n_dom, n_rot, particles, assign, rot_index, group, ctf_table):
    count = particles.shape[0]
    total = 8 * n_rot
    share = count // n_rot
    lanes = CYCLES // n_rot * MFREQ // 4
    half = 4 * lanes
    per_row = lanes // 128
    classes = CLS * n_dom
    vmem = pl.BlockSpec(memory_space=pltpu.VMEM)
    dma = pltpu.SemaphoreType.DMA
    parts, rot = dma((per_row, n_dom - 1)), dma((n_rot - 1,))
    shapes = (
        jax.ShapeDtypeStruct((CLS, K), BF16),
        jax.ShapeDtypeStruct((share, classes), F32),
    )
    results = pl.pallas_call(
        functools.partial(kernel, n_dom, n_rot),
        out_shape=shapes,
        in_specs=[pl.BlockSpec(memory_space=pltpu.HBM)] * 6,
        out_specs=(vmem, vmem),
        scratch_shapes=[
            pltpu.VMEM((2, count, half), BF16),
            pltpu.VMEM((1, count), jnp.int32),
            pltpu.VMEM((1, count), jnp.int32),
            pltpu.VMEM((1, count), jnp.int32),
            pltpu.VMEM(ctf_table.shape, F32),
            pltpu.VMEM((total, 256), F32),
            pltpu.VMEM((per_row, n_dom * (ROWS + 8), 128), F32),
            pltpu.VMEM((n_dom - 1, per_row, ROWS + 8, 128), F32),
            pltpu.VMEM((per_row, n_dom, ROWS, 128), BF16),
            pltpu.VMEM((per_row, n_dom * ROWS, 128), F32),
            pltpu.VMEM((8, 128), F32),
            pltpu.VMEM((n_rot - 1, 8, 128), F32),
            pltpu.VMEM((n_rot, per_row, ROWS, 128), BF16),
            pltpu.VMEM((per_row, n_rot * 128, 1024), BF16),
            pltpu.VMEM((per_row, FINE * classes, 1024), BF16),
            pltpu.VMEM((n_rot, FINE * classes, 128), F32),
            pltpu.VMEM((n_rot - 1, FINE * classes, 128), BF16),
            pltpu.VMEM((n_rot - 1, FINE * classes, 128), BF16),
            pltpu.VMEM((8, classes), F32),
            pltpu.VMEM((n_rot - 1, 8, classes), F32),
            dma((7,)),
            parts, parts, parts, parts, rot, rot, rot, rot, rot, rot, rot, rot,
        ],
        compiler_params=pltpu.CompilerParams(
            collective_id=0, has_side_effects=True, vmem_limit_bytes=48 * 1024 * 1024
        ),
    )(
        *(
            pltpu.with_memory_space_constraint(x, pltpu.HBM)
            for x in (
                particles,
                assign.reshape(1, count),
                rot_index.reshape(1, count),
                group.reshape(1, count),
                ctf_table,
                jnp.asarray(trig_table(total)),
            )
        )
    )
    return pl.pallas_call(
        write_out,
        out_shape=shapes,
        in_specs=[vmem, vmem],
        out_specs=[pl.BlockSpec(memory_space=pltpu.HBM)] * 2,
        scratch_shapes=[dma((2,))],
    )(*results)


def solution(mesh):
    sizes = dict(mesh.shape)
    in_specs = (P("dom", None), P("dom"), P("dom"), P("dom"), P())
    out_specs = (P("dom", None), P(("dom", "rot"), None))
    return jax.shard_map(
        functools.partial(local, sizes["dom"], sizes["rot"]),
        mesh=mesh, in_specs=in_specs, out_specs=out_specs, check_vma=False,
    )
```

```python
import functools
import math

import jax
import jax.numpy as jnp
import numpy as np
from jax import lax
from jax.experimental import pallas as pl
from jax.experimental.pallas import tpu as pltpu
from jax.sharding import PartitionSpec as P

CYCLES = 64
MFREQ = 64
CLS = 6
BLOCKS = 8
ROWS = BLOCKS * CLS
FINE = 4
K = 2 * CYCLES * MFREQ
MESH = pl.DeviceIdType.MESH
F32 = jnp.float32
BF16 = jnp.bfloat16


def pieces(x):
    high = x.astype(BF16)
    rest = x - high.astype(F32)
    mid = rest.astype(BF16)
    low = (rest - mid.astype(F32)).astype(BF16)
    return high, mid, low


def stacked(x):
    return jnp.concatenate(pieces(x), axis=0)


def iota(shape, dim):
    return lax.broadcasted_iota(jnp.int32, shape, dim)


def ones_where(cond):
    return jnp.where(cond, 1.0, 0.0).astype(BF16)


def dot(x, y):
    return jnp.dot(x, y, preferred_element_type=F32)


def column_onehot(row, count):
    shape = (3 * count, row.shape[1])
    return jnp.where((iota(shape, 0) & (count - 1)) == row, 1.0, 0.0).T.astype(BF16)


def each_row(tile):
    return jnp.concatenate([jnp.broadcast_to(tile[c : c + 1], (8, 128)) for c in range(CLS)], axis=0)


def kernel(
    n_dom, n_rot,
    particles_hbm, assign_hbm, rot_hbm, group_hbm, table_hbm, trig_hbm,
    refs_ref, scores_ref,
    spec, assign_ref, rot_ref, group_ref, table_ref, trig_ref,
    sums, other_core, sums_in, plain_all, wide, spread_mine, spread_in, normed, left, right,
    earlier, outgoing, incoming, norm_mine, norm_in,
    load_sem, p_send, p_recv, a_send, a_recv, c_send, c_recv, s_send, s_recv, r_send, r_recv,
    e_send, e_recv, n_send, n_recv,
):
    me = lax.axis_index("dom")
    zed = lax.axis_index("rot")
    count = spec.shape[1]
    total = trig_ref.shape[0]
    share = count // n_rot
    coarse = total // FINE
    cyc = CYCLES // n_rot
    half = cyc * MFREQ
    lanes = half // 4
    per_row = lanes // 128
    classes = CLS * n_dom
    deep = per_row * 24 + 8
    groups = table_ref.shape[0]

    barrier = pltpu.get_barrier_semaphore()

    def dom_peer(step):
        return (lax.rem(me + step, n_dom), zed)

    def rot_peer(step):
        return (me, lax.rem(zed + step, n_rot))

    for step in range(1, n_dom):
        pl.semaphore_signal(barrier, inc=1, device_id=dom_peer(step), device_id_type=MESH)
    for step in range(1, n_rot):
        pl.semaphore_signal(barrier, inc=1, device_id=rot_peer(step), device_id_type=MESH)

    pairs = [(group_hbm, group_ref), (table_hbm, table_ref), (rot_hbm, rot_ref)]
    pairs += [(trig_hbm, trig_ref), (assign_hbm, assign_ref)]
    for part in range(2):
        start = pl.multiple_of(part * CYCLES * MFREQ + zed * half, 128)
        pairs.append((particles_hbm.at[:, pl.ds(start, half)], spec.at[part]))
    loads = [pltpu.make_async_copy(x, y, load_sem.at[i]) for i, (x, y) in enumerate(pairs)]
    for load in loads:
        load.start()

    shape = (3 * CYCLES, half)
    spreader = ones_where((iota(shape, 0) & (CYCLES - 1)) == zed * cyc + iota(shape, 1) // MFREQ)
    loads[0].wait()
    loads[1].wait()
    rows = dot(column_onehot(group_ref[...], groups), stacked(table_ref[...]))
    factors = dot(jnp.concatenate(pieces(rows), axis=1), spreader)
    loads[2].wait()
    loads[3].wait()
    turns = dot(column_onehot(rot_ref[...], total), stacked(trig_ref[...]))
    cosine, sine = turns[:, :128], turns[:, 128:]

    loads[4].wait()
    labels = jnp.concatenate([assign_ref[...]] * 3, axis=1)
    place = iota((classes, 3 * count), 0)
    member = ones_where((place & (n_dom - 1)) * CLS + place // n_dom == labels)
    denom = dot(member, stacked(rows * rows))
    denom = jnp.concatenate([denom, jnp.zeros((classes, 128 - CYCLES), F32)], axis=1)

    def place_rows(c, r, values):
        at = pl.ds(r, n_dom, stride=deep)
        sums[c // 3, at, :] = values[c * n_dom : c * n_dom + n_dom]

    for c in range(CLS):
        place_rows(c, per_row * 24 + c % 3, denom)

    def lane_tile(block, part):
        first = block * lanes + part * 128
        return slice(first, first + 128)

    loads[5].wait()
    loads[6].wait()
    for part in range(per_row):
        for block in range(4):
            lane = lane_tile(block, part)
            re = spec[0, :, lane].astype(F32)
            im = spec[1, :, lane].astype(F32)
            both = [re * cosine + im * sine, im * cosine - re * sine]
            value = jnp.concatenate([x * factors[:, lane] for x in both], axis=1)
            numer = dot(member, stacked(value))
            for c in range(CLS):
                for i in range(2):
                    row = part * 24 + c % 3 * 8 + i * 4 + block
                    place_rows(c, row, numer[:, i * 128 : i * 128 + 128])

    pl.semaphore_wait(barrier, n_dom + n_rot - 2)
    core = lax.rem(me, 2)
    chip = me // 2
    swap = pltpu.make_async_remote_copy(
        src_ref=sums.at[1 - core],
        dst_ref=other_core,
        send_sem=p_send,
        recv_sem=p_recv,
        device_id=(me + 1 - 2 * core, zed),
        device_id_type=MESH,
    )
    swap.start()

    def turn_particles(part):
        for block in range(4):
            lane = lane_tile(block, part)
            re = (spec[0, :, lane].astype(F32) * factors[:, lane]).astype(BF16).astype(F32)
            im = (spec[1, :, lane].astype(F32) * factors[:, lane]).astype(BF16).astype(F32)
            turned_re, turned_im = [], []
            for a in range(coarse):
                cos = trig_ref[a * FINE : a * FINE + 1, :128]
                sin = trig_ref[a * FINE : a * FINE + 1, 128:]
                turned_re.append(re * cos + im * sin)
                turned_im.append(im * cos - re * sin)
            for i, turned in enumerate((turned_re, turned_im)):
                first = (i * 4 + block) * 128
                for z in range(n_rot):
                    left[part, z * 128 : z * 128 + 128, first : first + 128] = jnp.concatenate(
                        [x[z * share : z * share + share] for x in turned], axis=0
                    ).astype(BF16)

    if per_row > 1:
        turn_particles(0)
    swap.wait_recv()
    sums[core] = sums[core] + other_core[...]

    def message(owner):
        return sums.at[core, pl.ds(pl.multiple_of(owner * deep, 8), deep), :]

    a_copies = []
    for step in range(n_dom // 2):
        for target in range(2) if step else [1 - core]:
            owner = lax.rem(chip + step, n_dom // 2) * 2 + target
            a_copies.append(
                pltpu.make_async_remote_copy(
                    src_ref=message(owner),
                    dst_ref=sums_in.at[core, step],
                    send_sem=a_send.at[len(a_copies)],
                    recv_sem=a_recv.at[core, step],
                    device_id=(owner, zed),
                    device_id_type=MESH,
                )
            )
    for copy in a_copies[1:] + a_copies[:1]:
        copy.start()
    sums_in[core, 0] = message(me)[...]
    for part in range(1 if per_row > 1 else 0, per_row):
        turn_particles(part)

    cb = cyc // 4
    offset = iota((ROWS, 128), 1) - zed * cyc
    low = (iota((ROWS, 128), 0) & 3) * cb
    shape = (3 * 128, lanes)
    spreader = ones_where((iota(shape, 0) & (cb - 1)) == iota(shape, 1) // MFREQ)

    for step in range(n_dom // 2):
        for source in range(2) if step else [1 - core]:
            pltpu.make_async_remote_copy(
                src_ref=sums_in.at[source, step],
                dst_ref=sums_in.at[source, step],
                send_sem=p_send,
                recv_sem=a_recv.at[source, step],
                device_id=(me + 1 - 2 * core, zed),
                device_id_type=MESH,
            ).wait_recv()
    whole = sums_in[:, 0]
    for step in range(1, n_dom // 2):
        whole = whole + sums_in[:, step]
    denom = jnp.concatenate(
        [
            jnp.broadcast_to(whole[c // 3, per_row * 24 + c % 3][None], (8, 128))
            for c in range(CLS)
        ],
        axis=0,
    )
    denom = jnp.where((offset >= low) & (offset < low + cb), denom, 0.0)
    denom = dot(jnp.concatenate(pieces(denom), axis=1), spreader) + 1.0

    c_copies = []
    plain = []
    for part in range(per_row):
        numer = jnp.concatenate([whole[i, part * 24 : part * 24 + 24] for i in range(2)], axis=0)
        plain.append(numer / denom[:, part * 128 : part * 128 + 128])
        plain_all[part, me] = plain[-1].astype(BF16)
        group_copies = []
        for step in range(1, n_dom):
            group_copies.append(
                pltpu.make_async_remote_copy(
                    src_ref=plain_all.at[part, me],
                    dst_ref=plain_all.at[part, me],
                    send_sem=c_send.at[part, step - 1],
                    recv_sem=c_recv.at[part, step - 1],
                    device_id=dom_peer(step),
                    device_id_type=MESH,
                )
            )
            group_copies[-1].start()
        c_copies.append(group_copies)

    squares = sum(jnp.sum((x * x).reshape(CLS, 8, 128), axis=1) for x in plain)
    squares = jnp.broadcast_to(jnp.sum(squares, axis=1, keepdims=True), (CLS, 128))
    spread_mine[...] = jnp.concatenate([squares, jnp.zeros((8 - CLS, 128), F32)], axis=0)
    s_copies = []
    for step in range(1, n_rot):
        s_copies.append(
            pltpu.make_async_remote_copy(
                src_ref=spread_mine,
                dst_ref=spread_in.at[step - 1],
                send_sem=s_send.at[step - 1],
                recv_sem=s_recv.at[step - 1],
                device_id=rot_peer(step),
                device_id_type=MESH,
            )
        )
        s_copies[-1].start()

    def turn_references(part):
        for copy in c_copies[part]:
            copy.wait_recv()
        wide[part] = plain_all[part].astype(F32).reshape(classes * 8, 128)
        blocks = [wide[part, pl.ds(block, classes, stride=8), :] for block in range(BLOCKS)]
        for fine in range(FINE):
            cos = trig_ref[fine : fine + 1, :128]
            sin = trig_ref[fine : fine + 1, 128:]
            at = slice(fine * classes, fine * classes + classes)
            for block in range(4):
                re, im = blocks[block], blocks[block + 4]
                lane = slice(block * 128, block * 128 + 128)
                right[part, at, lane] = (re * cos - im * sin).astype(BF16)
                lane = slice(block * 128 + 512, block * 128 + 640)
                right[part, at, lane] = (re * sin + im * cos).astype(BF16)

    def product(part, rows):
        return lax.dot_general(
            right[part], rows, (((1,), (1,)), ((), ())), preferred_element_type=F32
        )

    for part in range(per_row - 1):
        turn_references(part)
        found = product(part, left[part])
        for z in range(n_rot):
            first = found[:, z * 128 : z * 128 + 128]
            earlier[z] = first if part == 0 else earlier[z] + first

    for copy in s_copies:
        copy.wait_recv()
    spread = spread_mine[...]
    for step in range(n_rot - 1):
        spread = spread + spread_in[step]
    root = each_row(jnp.sqrt(spread / K + 1e-6))
    for part in range(per_row):
        normed[zed, part] = (plain[part] / root).astype(BF16)
    r_copies = []
    for step in range(1, n_rot):
        r_copies.append(
            pltpu.make_async_remote_copy(
                src_ref=normed.at[zed],
                dst_ref=normed.at[zed],
                send_sem=r_send.at[step - 1],
                recv_sem=r_recv.at[step - 1],
                device_id=rot_peer(step),
                device_id_type=MESH,
            )
        )
        r_copies[-1].start()

    last = per_row - 1
    turn_references(last)

    def partial(z):
        rows = left[last, pl.ds(pl.multiple_of(z * 128, 128), 128), :]
        return product(last, rows) + earlier[z] if last else product(last, rows)

    steps = [n_rot // 2]
    for step in range(n_rot // 2 - 1, 0, -1):
        steps += [lax.select(zed % 2 == 0, n_rot - step, step)]
        steps += [lax.select(zed % 2 == 0, step, n_rot - step)]
    e_copies = []
    for i, step in enumerate(steps):
        outgoing[i] = partial(lax.rem(zed + step, n_rot)).astype(BF16)
        e_copies.append(
            pltpu.make_async_remote_copy(
                src_ref=outgoing.at[i],
                dst_ref=incoming.at[i],
                send_sem=e_send.at[i],
                recv_sem=e_recv.at[i],
                device_id=rot_peer(step),
                device_id_type=MESH,
            )
        )
        e_copies[-1].start()

    squares = jnp.zeros((classes, 128), F32)
    for part in range(per_row):
        for block in range(BLOCKS):
            x = wide[part, pl.ds(block, classes, stride=8), :]
            squares = squares + x * x
    squares = jnp.broadcast_to(jnp.sum(squares, axis=1, keepdims=True), (classes, 128))
    norm_mine[...] = squares.T[:8]
    n_copies = []
    for step in range(1, n_rot):
        n_copies.append(
            pltpu.make_async_remote_copy(
                src_ref=norm_mine,
                dst_ref=norm_in.at[step - 1],
                send_sem=n_send.at[step - 1],
                recv_sem=n_recv.at[step - 1],
                device_id=rot_peer(step),
                device_id_type=MESH,
            )
        )
        n_copies[-1].start()
    found = partial(zed)

    for copy in r_copies:
        copy.wait_recv()
    for z in range(n_rot):
        for part in range(per_row):
            wide[part, :ROWS] = normed[z, part].astype(F32)
            for block in range(BLOCKS):
                first = (block // 4) * CYCLES * MFREQ + z * half
                first += (block % 4) * lanes + part * 128
                values = wide[part, pl.ds(block, CLS, stride=8), :]
                refs_ref[:, first : first + 128] = values.astype(BF16)

    for copy in n_copies:
        copy.wait_recv()
    spread = norm_mine[...]
    for step in range(n_rot - 1):
        spread = spread + norm_in[step]
    scale = (1.0 / math.sqrt(K)) / jnp.sqrt(spread / K + 1e-6)

    for i, copy in enumerate(e_copies):
        copy.wait_recv()
        found = found + incoming[i].astype(F32)
    best = found[:classes]
    for fine in range(1, FINE):
        best = jnp.maximum(best, found[fine * classes : fine * classes + classes])
    best = best.T
    top = best[:share]
    for a in range(1, coarse):
        top = jnp.maximum(top, best[a * share : a * share + share])
    scores_ref[...] = top * scale[:1]

    for copy in [swap] + a_copies + sum(c_copies, []) + s_copies + r_copies + e_copies + n_copies:
        copy.wait_send()


def trig_table(total):
    freqs = np.arange(128) % MFREQ
    phase = (np.arange(total)[:, None] * freqs[None, :]) % total * (2.0 * math.pi / total)
    return np.concatenate([np.cos(phase), np.sin(phase)], axis=1).astype(np.float32)


def local(n_dom, n_rot, particles, assign, rot_index, group, ctf_table):
    count = particles.shape[0]
    total = 8 * n_rot
    share = count // n_rot
    lanes = CYCLES // n_rot * MFREQ // 4
    half = 4 * lanes
    per_row = lanes // 128
    classes = CLS * n_dom
    vmem = pl.BlockSpec(memory_space=pltpu.VMEM)
    dma = pltpu.SemaphoreType.DMA
    deep = per_row * 24 + 8
    parts, rot = dma((per_row, n_dom - 1)), dma((n_rot - 1,))
    shapes = (
        jax.ShapeDtypeStruct((CLS, K), BF16),
        jax.ShapeDtypeStruct((share, classes), F32),
    )
    return pl.pallas_call(
        functools.partial(kernel, n_dom, n_rot),
        out_shape=shapes,
        in_specs=[pl.BlockSpec(memory_space=pltpu.HBM)] * 6,
        out_specs=(vmem, vmem),
        scratch_shapes=[
            pltpu.VMEM((2, count, half), BF16),
            pltpu.VMEM((1, count), jnp.int32),
            pltpu.VMEM((1, count), jnp.int32),
            pltpu.VMEM((1, count), jnp.int32),
            pltpu.VMEM(ctf_table.shape, F32),
            pltpu.VMEM((total, 256), F32),
            pltpu.VMEM((2, n_dom * deep, 128), F32),
            pltpu.VMEM((n_dom * deep, 128), F32),
            pltpu.VMEM((2, n_dom // 2, deep, 128), F32),
            pltpu.VMEM((per_row, n_dom, ROWS, 128), BF16),
            pltpu.VMEM((per_row, n_dom * ROWS, 128), F32),
            pltpu.VMEM((8, 128), F32),
            pltpu.VMEM((n_rot - 1, 8, 128), F32),
            pltpu.VMEM((n_rot, per_row, ROWS, 128), BF16),
            pltpu.VMEM((per_row, n_rot * 128, 1024), BF16),
            pltpu.VMEM((per_row, FINE * classes, 1024), BF16),
            pltpu.VMEM((n_rot, FINE * classes, 128), F32),
            pltpu.VMEM((n_rot - 1, FINE * classes, 128), BF16),
            pltpu.VMEM((n_rot - 1, FINE * classes, 128), BF16),
            pltpu.VMEM((8, classes), F32),
            pltpu.VMEM((n_rot - 1, 8, classes), F32),
            dma((7,)), dma(()), dma(()),
            dma((n_dom - 1,)), dma((2, n_dom // 2)), parts, parts, rot, rot, rot, rot, rot, rot, rot, rot,
        ],
        compiler_params=pltpu.CompilerParams(
            collective_id=0, has_side_effects=True, vmem_limit_bytes=48 * 1024 * 1024
        ),
    )(
        *(
            pltpu.with_memory_space_constraint(x, pltpu.HBM)
            for x in (
                particles,
                assign.reshape(1, count),
                rot_index.reshape(1, count),
                group.reshape(1, count),
                ctf_table,
                jnp.asarray(trig_table(total)),
            )
        )
    )


def solution(mesh):
    sizes = dict(mesh.shape)
    in_specs = (P("dom", None), P("dom"), P("dom"), P("dom"), P())
    out_specs = (P("dom", None), P(("dom", "rot"), None))
    return jax.shard_map(
        functools.partial(local, sizes["dom"], sizes["rot"]),
        mesh=mesh, in_specs=in_specs, out_specs=out_specs, check_vma=False,
    )
```

```python
import functools
import math

import jax
import jax.numpy as jnp
import numpy as np
from jax import lax
from jax.experimental import pallas as pl
from jax.experimental.pallas import tpu as pltpu
from jax.sharding import PartitionSpec as P

CYCLES = 64
MFREQ = 64
CLS = 6
BLOCKS = 8
ROWS = BLOCKS * CLS
FINE = 4
K = 2 * CYCLES * MFREQ
MESH = pl.DeviceIdType.MESH
F32 = jnp.float32
BF16 = jnp.bfloat16


def pieces(x):
    high = x.astype(BF16)
    rest = x - high.astype(F32)
    mid = rest.astype(BF16)
    low = (rest - mid.astype(F32)).astype(BF16)
    return high, mid, low


def stacked(x):
    return jnp.concatenate(pieces(x), axis=0)


def iota(shape, dim):
    return lax.broadcasted_iota(jnp.int32, shape, dim)


def ones_where(cond):
    return jnp.where(cond, 1.0, 0.0).astype(BF16)


def dot(x, y):
    return jnp.dot(x, y, preferred_element_type=F32)


def column_onehot(row, count):
    shape = (3 * count, row.shape[1])
    return jnp.where((iota(shape, 0) & (count - 1)) == row, 1.0, 0.0).T.astype(BF16)


def each_row(tile):
    return jnp.concatenate([jnp.broadcast_to(tile[c : c + 1], (8, 128)) for c in range(CLS)], axis=0)


def kernel(
    n_dom, n_rot,
    particles_hbm, assign_hbm, rot_hbm, group_hbm, table_hbm, trig_hbm,
    refs_ref, scores_ref,
    spec, assign_ref, rot_ref, group_ref, table_ref, trig_ref,
    sums, sums_in, plain_all, wide, spread_mine, spread_in, normed, left, right,
    earlier, outgoing, incoming, norm_mine, norm_in,
    load_sem, a_send, a_recv, c_send, c_recv, s_send, s_recv, r_send, r_recv,
    e_send, e_recv, n_send, n_recv,
):
    me = lax.axis_index("dom")
    zed = lax.axis_index("rot")
    count = spec.shape[1]
    total = trig_ref.shape[0]
    share = count // n_rot
    coarse = total // FINE
    cyc = CYCLES // n_rot
    half = cyc * MFREQ
    lanes = half // 4
    per_row = lanes // 128
    classes = CLS * n_dom
    groups = table_ref.shape[0]

    barrier = pltpu.get_barrier_semaphore()

    def dom_peer(step):
        return (lax.rem(me + step, n_dom), zed)

    def rot_peer(step):
        return (me, lax.rem(zed + step, n_rot))

    for step in range(1, n_dom):
        pl.semaphore_signal(barrier, inc=1, device_id=dom_peer(step), device_id_type=MESH)
    for step in range(1, n_rot):
        pl.semaphore_signal(barrier, inc=1, device_id=rot_peer(step), device_id_type=MESH)

    pairs = [(group_hbm, group_ref), (table_hbm, table_ref), (rot_hbm, rot_ref)]
    pairs += [(trig_hbm, trig_ref), (assign_hbm, assign_ref)]
    for part in range(2):
        start = pl.multiple_of(part * CYCLES * MFREQ + zed * half, 128)
        pairs.append((particles_hbm.at[:, pl.ds(start, half)], spec.at[part]))
    loads = [pltpu.make_async_copy(x, y, load_sem.at[i]) for i, (x, y) in enumerate(pairs)]
    for load in loads:
        load.start()

    shape = (3 * CYCLES, half)
    spreader = ones_where((iota(shape, 0) & (CYCLES - 1)) == zed * cyc + iota(shape, 1) // MFREQ)
    loads[0].wait()
    loads[1].wait()
    rows = dot(column_onehot(group_ref[...], groups), stacked(table_ref[...]))
    factors = dot(jnp.concatenate(pieces(rows), axis=1), spreader)
    loads[2].wait()
    loads[3].wait()
    turns = dot(column_onehot(rot_ref[...], total), stacked(trig_ref[...]))
    cosine, sine = turns[:, :128], turns[:, 128:]

    loads[4].wait()
    labels = jnp.concatenate([assign_ref[...]] * 3, axis=1)
    place = iota((classes, 3 * count), 0)
    member = ones_where((place & (n_dom - 1)) * CLS + place // n_dom == labels)
    denom = dot(member, stacked(rows * rows))
    denom = jnp.concatenate([denom, jnp.zeros((classes, 128 - CYCLES), F32)], axis=1)
    for c in range(CLS):
        at = pl.ds(ROWS + c, n_dom, stride=ROWS + 8)
        sums[0, at, :] = denom[c * n_dom : c * n_dom + n_dom]

    def message(part, owner):
        first = pl.multiple_of(owner * (ROWS + 8), 8)
        return sums.at[part, pl.ds(first, ROWS + 8 if part == 0 else ROWS), :]

    def landing(part, step):
        return sums_in.at[step - 1, part, pl.ds(0, ROWS + 8 if part == 0 else ROWS), :]

    def lane_tile(block, part):
        first = block * lanes + part * 128
        return slice(first, first + 128)

    loads[5].wait()
    loads[6].wait()
    a_copies = []
    for part in range(per_row):
        for block in range(4):
            lane = lane_tile(block, part)
            re = spec[0, :, lane].astype(F32)
            im = spec[1, :, lane].astype(F32)
            both = [re * cosine + im * sine, im * cosine - re * sine]
            value = jnp.concatenate([x * factors[:, lane] for x in both], axis=1)
            numer = dot(member, stacked(value))
            for c in range(CLS):
                for i in range(2):
                    at = pl.ds(c * 8 + i * 4 + block, n_dom, stride=ROWS + 8)
                    sums[part, at, :] = numer[
                        c * n_dom : c * n_dom + n_dom, i * 128 : i * 128 + 128
                    ]
        if part == 0:
            pl.semaphore_wait(barrier, n_dom + n_rot - 2)
        group_copies = []
        for step in range(1, n_dom):
            group_copies.append(
                pltpu.make_async_remote_copy(
                    src_ref=message(part, lax.rem(me + step, n_dom)),
                    dst_ref=landing(part, step),
                    send_sem=a_send.at[part, step - 1],
                    recv_sem=a_recv.at[part, step - 1],
                    device_id=dom_peer(step),
                    device_id_type=MESH,
                )
            )
            group_copies[-1].start()
        a_copies.append(group_copies)

    for part in range(per_row):
        for block in range(4):
            lane = lane_tile(block, part)
            re = (spec[0, :, lane].astype(F32) * factors[:, lane]).astype(BF16).astype(F32)
            im = (spec[1, :, lane].astype(F32) * factors[:, lane]).astype(BF16).astype(F32)
            turned_re, turned_im = [], []
            for a in range(coarse):
                cos = trig_ref[a * FINE : a * FINE + 1, :128]
                sin = trig_ref[a * FINE : a * FINE + 1, 128:]
                turned_re.append(re * cos + im * sin)
                turned_im.append(im * cos - re * sin)
            for i, turned in enumerate((turned_re, turned_im)):
                first = (i * 4 + block) * 128
                for z in range(n_rot):
                    left[part, z * 128 : z * 128 + 128, first : first + 128] = jnp.concatenate(
                        [x[z * share : z * share + share] for x in turned], axis=0
                    ).astype(BF16)

    cb = cyc // 4
    offset = iota((ROWS, 128), 1) - zed * cyc
    low = (iota((ROWS, 128), 0) & 3) * cb
    shape = (3 * 128, lanes)
    spreader = ones_where((iota(shape, 0) & (cb - 1)) == iota(shape, 1) // MFREQ)

    c_copies = []
    plain = []
    for part in range(per_row):
        for copy in a_copies[part]:
            copy.wait_recv()
        whole = message(part, me)[...]
        for step in range(1, n_dom):
            whole = whole + landing(part, step)[...]
        if part == 0:
            denom = jnp.where(
                (offset >= low) & (offset < low + cb), each_row(whole[ROWS:]), 0.0
            )
            denom = dot(jnp.concatenate(pieces(denom), axis=1), spreader) + 1.0
        plain.append(whole[:ROWS] / denom[:, part * 128 : part * 128 + 128])
        plain_all[part, me] = plain[-1].astype(BF16)
        group_copies = []
        for step in range(1, n_dom):
            group_copies.append(
                pltpu.make_async_remote_copy(
                    src_ref=plain_all.at[part, me],
                    dst_ref=plain_all.at[part, me],
                    send_sem=c_send.at[part, step - 1],
                    recv_sem=c_recv.at[part, step - 1],
                    device_id=dom_peer(step),
                    device_id_type=MESH,
                )
            )
            group_copies[-1].start()
        c_copies.append(group_copies)

    squares = sum(jnp.sum((x * x).reshape(CLS, 8, 128), axis=1) for x in plain)
    squares = jnp.broadcast_to(jnp.sum(squares, axis=1, keepdims=True), (CLS, 128))
    spread_mine[...] = jnp.concatenate([squares, jnp.zeros((8 - CLS, 128), F32)], axis=0)
    s_copies = []
    for step in range(1, n_rot):
        s_copies.append(
            pltpu.make_async_remote_copy(
                src_ref=spread_mine,
                dst_ref=spread_in.at[step - 1],
                send_sem=s_send.at[step - 1],
                recv_sem=s_recv.at[step - 1],
                device_id=rot_peer(step),
                device_id_type=MESH,
            )
        )
        s_copies[-1].start()

    def turn_references(part):
        for copy in c_copies[part]:
            copy.wait_recv()
        wide[part] = plain_all[part].astype(F32).reshape(classes * 8, 128)
        blocks = [wide[part, pl.ds(block, classes, stride=8), :] for block in range(BLOCKS)]
        for fine in range(FINE):
            cos = trig_ref[fine : fine + 1, :128]
            sin = trig_ref[fine : fine + 1, 128:]
            at = slice(fine * classes, fine * classes + classes)
            for block in range(4):
                re, im = blocks[block], blocks[block + 4]
                lane = slice(block * 128, block * 128 + 128)
                right[part, at, lane] = (re * cos - im * sin).astype(BF16)
                lane = slice(block * 128 + 512, block * 128 + 640)
                right[part, at, lane] = (re * sin + im * cos).astype(BF16)

    def product(part, rows):
        return lax.dot_general(
            right[part], rows, (((1,), (1,)), ((), ())), preferred_element_type=F32
        )

    for part in range(per_row - 1):
        turn_references(part)
        found = product(part, left[part])
        for z in range(n_rot):
            first = found[:, z * 128 : z * 128 + 128]
            earlier[z] = first if part == 0 else earlier[z] + first

    for copy in s_copies:
        copy.wait_recv()
    spread = spread_mine[...]
    for step in range(n_rot - 1):
        spread = spread + spread_in[step]
    root = each_row(jnp.sqrt(spread / K + 1e-6))
    for part in range(per_row):
        normed[zed, part] = (plain[part] / root).astype(BF16)
    r_copies = []
    for step in range(1, n_rot):
        r_copies.append(
            pltpu.make_async_remote_copy(
                src_ref=normed.at[zed],
                dst_ref=normed.at[zed],
                send_sem=r_send.at[step - 1],
                recv_sem=r_recv.at[step - 1],
                device_id=rot_peer(step),
                device_id_type=MESH,
            )
        )
        r_copies[-1].start()

    last = per_row - 1
    turn_references(last)

    def partial(z):
        rows = left[last, pl.ds(pl.multiple_of(z * 128, 128), 128), :]
        return product(last, rows) + earlier[z] if last else product(last, rows)

    steps = [n_rot // 2]
    for step in range(n_rot // 2 - 1, 0, -1):
        steps += [lax.select(zed % 2 == 0, n_rot - step, step)]
        steps += [lax.select(zed % 2 == 0, step, n_rot - step)]
    e_copies = []
    for i, step in enumerate(steps):
        outgoing[i] = partial(lax.rem(zed + step, n_rot)).astype(BF16)
        e_copies.append(
            pltpu.make_async_remote_copy(
                src_ref=outgoing.at[i],
                dst_ref=incoming.at[i],
                send_sem=e_send.at[i],
                recv_sem=e_recv.at[i],
                device_id=rot_peer(step),
                device_id_type=MESH,
            )
        )
        e_copies[-1].start()

    squares = jnp.zeros((classes, 128), F32)
    for part in range(per_row):
        for block in range(BLOCKS):
            x = wide[part, pl.ds(block, classes, stride=8), :]
            squares = squares + x * x
    squares = jnp.broadcast_to(jnp.sum(squares, axis=1, keepdims=True), (classes, 128))
    norm_mine[...] = squares.T[:8]
    n_copies = []
    for step in range(1, n_rot):
        n_copies.append(
            pltpu.make_async_remote_copy(
                src_ref=norm_mine,
                dst_ref=norm_in.at[step - 1],
                send_sem=n_send.at[step - 1],
                recv_sem=n_recv.at[step - 1],
                device_id=rot_peer(step),
                device_id_type=MESH,
            )
        )
        n_copies[-1].start()
    found = partial(zed)

    for copy in r_copies:
        copy.wait_recv()
    for z in range(n_rot):
        for part in range(per_row):
            wide[part, :ROWS] = normed[z, part].astype(F32)
            for block in range(BLOCKS):
                first = (block // 4) * CYCLES * MFREQ + z * half
                first += (block % 4) * lanes + part * 128
                values = wide[part, pl.ds(block, CLS, stride=8), :]
                refs_ref[:, first : first + 128] = values.astype(BF16)

    for copy in n_copies:
        copy.wait_recv()
    spread = norm_mine[...]
    for step in range(n_rot - 1):
        spread = spread + norm_in[step]
    scale = (1.0 / math.sqrt(K)) / jnp.sqrt(spread / K + 1e-6)

    for i, copy in enumerate(e_copies):
        copy.wait_recv()
        found = found + incoming[i].astype(F32)
    best = found[:classes]
    for fine in range(1, FINE):
        best = jnp.maximum(best, found[fine * classes : fine * classes + classes])
    best = best.T
    top = best[:share]
    for a in range(1, coarse):
        top = jnp.maximum(top, best[a * share : a * share + share])
    scores_ref[...] = top * scale[:1]

    for copy in sum(a_copies + c_copies, []) + s_copies + r_copies + e_copies + n_copies:
        copy.wait_send()


def trig_table(total):
    freqs = np.arange(128) % MFREQ
    phase = (np.arange(total)[:, None] * freqs[None, :]) % total * (2.0 * math.pi / total)
    return np.concatenate([np.cos(phase), np.sin(phase)], axis=1).astype(np.float32)


def local(n_dom, n_rot, particles, assign, rot_index, group, ctf_table):
    count = particles.shape[0]
    total = 8 * n_rot
    share = count // n_rot
    lanes = CYCLES // n_rot * MFREQ // 4
    half = 4 * lanes
    per_row = lanes // 128
    classes = CLS * n_dom
    vmem = pl.BlockSpec(memory_space=pltpu.VMEM)
    dma = pltpu.SemaphoreType.DMA
    parts, rot = dma((per_row, n_dom - 1)), dma((n_rot - 1,))
    shapes = (
        jax.ShapeDtypeStruct((CLS, K), BF16),
        jax.ShapeDtypeStruct((share, classes), F32),
    )
    return pl.pallas_call(
        functools.partial(kernel, n_dom, n_rot),
        out_shape=shapes,
        in_specs=[pl.BlockSpec(memory_space=pltpu.HBM)] * 6,
        out_specs=(vmem, vmem),
        scratch_shapes=[
            pltpu.VMEM((2, count, half), BF16),
            pltpu.VMEM((1, count), jnp.int32),
            pltpu.VMEM((1, count), jnp.int32),
            pltpu.VMEM((1, count), jnp.int32),
            pltpu.VMEM(ctf_table.shape, F32),
            pltpu.VMEM((total, 256), F32),
            pltpu.VMEM((per_row, n_dom * (ROWS + 8), 128), F32),
            pltpu.VMEM((n_dom - 1, per_row, ROWS + 8, 128), F32),
            pltpu.VMEM((per_row, n_dom, ROWS, 128), BF16),
            pltpu.VMEM((per_row, n_dom * ROWS, 128), F32),
            pltpu.VMEM((8, 128), F32),
            pltpu.VMEM((n_rot - 1, 8, 128), F32),
            pltpu.VMEM((n_rot, per_row, ROWS, 128), BF16),
            pltpu.VMEM((per_row, n_rot * 128, 1024), BF16),
            pltpu.VMEM((per_row, FINE * classes, 1024), BF16),
            pltpu.VMEM((n_rot, FINE * classes, 128), F32),
            pltpu.VMEM((n_rot - 1, FINE * classes, 128), BF16),
            pltpu.VMEM((n_rot - 1, FINE * classes, 128), BF16),
            pltpu.VMEM((8, classes), F32),
            pltpu.VMEM((n_rot - 1, 8, classes), F32),
            dma((7,)),
            parts, parts, parts, parts, rot, rot, rot, rot, rot, rot, rot, rot,
        ],
        compiler_params=pltpu.CompilerParams(
            collective_id=0, has_side_effects=True, vmem_limit_bytes=48 * 1024 * 1024
        ),
    )(
        *(
            pltpu.with_memory_space_constraint(x, pltpu.HBM)
            for x in (
                particles,
                assign.reshape(1, count),
                rot_index.reshape(1, count),
                group.reshape(1, count),
                ctf_table,
                jnp.asarray(trig_table(total)),
            )
        )
    )


def solution(mesh):
    sizes = dict(mesh.shape)
    in_specs = (P("dom", None), P("dom"), P("dom"), P("dom"), P())
    out_specs = (P("dom", None), P(("dom", "rot"), None))
    return jax.shard_map(
        functools.partial(local, sizes["dom"], sizes["rot"]),
        mesh=mesh, in_specs=in_specs, out_specs=out_specs, check_vma=False,
    )
```

```python
import functools
import math

import jax
import jax.numpy as jnp
import numpy as np
from jax import lax
from jax.experimental import pallas as pl
from jax.experimental.pallas import tpu as pltpu
from jax.sharding import PartitionSpec as P

CYCLES = 64
MFREQ = 64
CLS = 6
BLOCKS = 8
ROWS = BLOCKS * CLS
FINE = 4
K = 2 * CYCLES * MFREQ
MESH = pl.DeviceIdType.MESH
F32 = jnp.float32
BF16 = jnp.bfloat16


def pieces(x):
    high = x.astype(BF16)
    rest = x - high.astype(F32)
    mid = rest.astype(BF16)
    low = (rest - mid.astype(F32)).astype(BF16)
    return high, mid, low


def stacked(x):
    return jnp.concatenate(pieces(x), axis=0)


def iota(shape, dim):
    return lax.broadcasted_iota(jnp.int32, shape, dim)


def ones_where(cond):
    return jnp.where(cond, 1.0, 0.0).astype(BF16)


def dot(x, y):
    return jnp.dot(x, y, preferred_element_type=F32)


def column_onehot(row, count):
    shape = (3 * count, row.shape[1])
    return jnp.where((iota(shape, 0) & (count - 1)) == row, 1.0, 0.0).T.astype(BF16)


def each_row(tile):
    return jnp.concatenate([jnp.broadcast_to(tile[c : c + 1], (8, 128)) for c in range(CLS)], axis=0)


def kernel(
    n_dom, n_rot,
    particles_hbm, assign_hbm, rot_hbm, group_hbm, table_hbm, trig_hbm,
    refs_ref, scores_ref,
    spec, assign_ref, rot_ref, group_ref, table_ref, trig_ref,
    sums, sums_in, plain_all, wide, spread_mine, spread_in, normed, left, right,
    square_rows, outgoing, incoming, norm_mine, norm_in,
    load_sem, a_send, a_recv, c_send, c_recv, s_send, s_recv, r_send, r_recv,
    e_send, e_recv, n_send, n_recv,
):
    me = lax.axis_index("dom")
    zed = lax.axis_index("rot")
    count = spec.shape[1]
    total = trig_ref.shape[0]
    share = count // n_rot
    coarse = total // FINE
    cyc = CYCLES // n_rot
    half = cyc * MFREQ
    lanes = half // 4
    per_row = lanes // 128
    classes = CLS * n_dom
    groups = table_ref.shape[0]

    barrier = pltpu.get_barrier_semaphore()

    def dom_peer(step):
        return (lax.rem(me + step, n_dom), zed)

    def rot_peer(step):
        return (me, lax.rem(zed + step, n_rot))

    for step in range(1, n_dom):
        pl.semaphore_signal(barrier, inc=1, device_id=dom_peer(step), device_id_type=MESH)
    for step in range(1, n_rot):
        pl.semaphore_signal(barrier, inc=1, device_id=rot_peer(step), device_id_type=MESH)

    pairs = [(group_hbm, group_ref), (table_hbm, table_ref), (rot_hbm, rot_ref)]
    pairs += [(trig_hbm, trig_ref), (assign_hbm, assign_ref)]
    for part in range(2):
        start = pl.multiple_of(part * CYCLES * MFREQ + zed * half, 128)
        pairs.append((particles_hbm.at[:, pl.ds(start, half)], spec.at[part]))
    loads = [pltpu.make_async_copy(x, y, load_sem.at[i]) for i, (x, y) in enumerate(pairs)]
    for load in loads:
        load.start()

    shape = (3 * CYCLES, half)
    spreader = ones_where((iota(shape, 0) & (CYCLES - 1)) == zed * cyc + iota(shape, 1) // MFREQ)
    loads[0].wait()
    loads[1].wait()
    rows = dot(column_onehot(group_ref[...], groups), stacked(table_ref[...]))
    factors = dot(jnp.concatenate(pieces(rows), axis=1), spreader)
    loads[2].wait()
    loads[3].wait()
    turns = dot(column_onehot(rot_ref[...], total), stacked(trig_ref[...]))
    cosine, sine = turns[:, :128], turns[:, 128:]

    loads[4].wait()
    labels = jnp.concatenate([assign_ref[...]] * 3, axis=1)
    place = iota((classes, 3 * count), 0)
    member = ones_where((place & (n_dom - 1)) * CLS + place // n_dom == labels)
    denom = dot(member, stacked(rows * rows))
    denom = jnp.concatenate([denom, jnp.zeros((classes, 128 - CYCLES), F32)], axis=1)
    for c in range(CLS):
        at = pl.ds(ROWS + c, n_dom, stride=ROWS + 8)
        sums[0, at, :] = denom[c * n_dom : c * n_dom + n_dom]

    def message(part, owner):
        first = pl.multiple_of(owner * (ROWS + 8), 8)
        return sums.at[part, pl.ds(first, ROWS + 8 if part == 0 else ROWS), :]

    def landing(part, step):
        return sums_in.at[step - 1, part, pl.ds(0, ROWS + 8 if part == 0 else ROWS), :]

    def lane_tile(block, part):
        first = block * lanes + part * 128
        return slice(first, first + 128)

    loads[5].wait()
    loads[6].wait()
    a_copies = []
    for part in range(per_row):
        for block in range(4):
            lane = lane_tile(block, part)
            re = spec[0, :, lane].astype(F32)
            im = spec[1, :, lane].astype(F32)
            both = [re * cosine + im * sine, im * cosine - re * sine]
            value = jnp.concatenate([x * factors[:, lane] for x in both], axis=1)
            numer = dot(member, stacked(value))
            for c in range(CLS):
                for i in range(2):
                    at = pl.ds(c * 8 + i * 4 + block, n_dom, stride=ROWS + 8)
                    sums[part, at, :] = numer[
                        c * n_dom : c * n_dom + n_dom, i * 128 : i * 128 + 128
                    ]
        if part == 0:
            pl.semaphore_wait(barrier, n_dom + n_rot - 2)
        group_copies = []
        for step in range(1, n_dom):
            group_copies.append(
                pltpu.make_async_remote_copy(
                    src_ref=message(part, lax.rem(me + step, n_dom)),
                    dst_ref=landing(part, step),
                    send_sem=a_send.at[part, step - 1],
                    recv_sem=a_recv.at[part, step - 1],
                    device_id=dom_peer(step),
                    device_id_type=MESH,
                )
            )
            group_copies[-1].start()
        a_copies.append(group_copies)

    for part in range(per_row):
        for block in range(4):
            lane = lane_tile(block, part)
            re = (spec[0, :, lane].astype(F32) * factors[:, lane]).astype(BF16).astype(F32)
            im = (spec[1, :, lane].astype(F32) * factors[:, lane]).astype(BF16).astype(F32)
            turned_re, turned_im = [], []
            for a in range(coarse):
                cos = trig_ref[a * FINE : a * FINE + 1, :128]
                sin = trig_ref[a * FINE : a * FINE + 1, 128:]
                turned_re.append(re * cos + im * sin)
                turned_im.append(im * cos - re * sin)
            for i, turned in enumerate((turned_re, turned_im)):
                first = part * 1024 + (i * 4 + block) * 128
                for z in range(n_rot):
                    left[z * 128 : z * 128 + 128, first : first + 128] = jnp.concatenate(
                        [x[z * share : z * share + share] for x in turned], axis=0
                    ).astype(BF16)

    cb = cyc // 4
    offset = iota((ROWS, 128), 1) - zed * cyc
    low = (iota((ROWS, 128), 0) & 3) * cb
    shape = (3 * 128, lanes)
    spreader = ones_where((iota(shape, 0) & (cb - 1)) == iota(shape, 1) // MFREQ)

    plain = []
    for part in range(per_row):
        for copy in a_copies[part]:
            copy.wait_recv()
        whole = message(part, me)[...]
        for step in range(1, n_dom):
            whole = whole + landing(part, step)[...]
        if part == 0:
            denom = jnp.where(
                (offset >= low) & (offset < low + cb), each_row(whole[ROWS:]), 0.0
            )
            denom = dot(jnp.concatenate(pieces(denom), axis=1), spreader) + 1.0
        plain.append(whole[:ROWS] / denom[:, part * 128 : part * 128 + 128])
        plain_all[me, part] = plain[-1].astype(BF16)

    many = n_dom // 2
    own_half = me // many
    halves = [own_half, 1 - own_half]
    spot = me - own_half * many
    c_copies = [[], []]
    for side in range(2):
        for step in range(1 - side, many):
            peer = halves[side] * many + lax.rem(spot + step, many)
            c_copies[side].append(
                pltpu.make_async_remote_copy(
                    src_ref=plain_all.at[me],
                    dst_ref=plain_all.at[me],
                    send_sem=c_send.at[side, step],
                    recv_sem=c_recv.at[side, step],
                    device_id=(peer, zed),
                    device_id_type=MESH,
                )
            )
            c_copies[side][-1].start()

    squares = sum(jnp.sum((x * x).reshape(CLS, 8, 128), axis=1) for x in plain)
    squares = jnp.broadcast_to(jnp.sum(squares, axis=1, keepdims=True), (CLS, 128))
    spread_mine[...] = jnp.concatenate([squares, jnp.zeros((8 - CLS, 128), F32)], axis=0)
    s_copies = []
    for step in range(1, n_rot):
        s_copies.append(
            pltpu.make_async_remote_copy(
                src_ref=spread_mine,
                dst_ref=spread_in.at[step - 1],
                send_sem=s_send.at[step - 1],
                recv_sem=s_recv.at[step - 1],
                device_id=rot_peer(step),
                device_id_type=MESH,
            )
        )
        s_copies[-1].start()

    some = classes // 2

    def turn_references(side):
        for copy in c_copies[side]:
            copy.wait_recv()
        squares = jnp.zeros((some, 128), F32)
        for part in range(per_row):
            mine = plain_all[pl.ds(halves[side] * many, many), part]
            wide[side, part] = mine.astype(F32).reshape(some * 8, 128)
            blocks = [wide[side, part, pl.ds(block, some, stride=8), :] for block in range(BLOCKS)]
            for block in blocks:
                squares = squares + block * block
            for fine in range(FINE):
                cos = trig_ref[fine : fine + 1, :128]
                sin = trig_ref[fine : fine + 1, 128:]
                at = slice(fine * some, fine * some + some)
                for block in range(4):
                    re, im = blocks[block], blocks[block + 4]
                    first = part * 1024 + block * 128
                    right[side, at, first : first + 128] = (re * cos - im * sin).astype(BF16)
                    first += 512
                    right[side, at, first : first + 128] = (re * sin + im * cos).astype(BF16)
        squares = jnp.broadcast_to(jnp.sum(squares, axis=1, keepdims=True), (some, 128))
        square_rows[pl.ds(pl.multiple_of(halves[side] * some, 8), some), :] = squares

    def partial(side, z):
        return lax.dot_general(
            right[side],
            left[pl.ds(pl.multiple_of(z * 128, 128), 128), :],
            (((1,), (1,)), ((), ())),
            preferred_element_type=F32,
        )

    steps = [n_rot // 2]
    for step in range(n_rot // 2 - 1, 0, -1):
        steps += [lax.select(zed % 2 == 0, n_rot - step, step)]
        steps += [lax.select(zed % 2 == 0, step, n_rot - step)]
    e_copies = []

    def send_partials(side):
        for i, step in enumerate(steps):
            outgoing[side, i] = partial(side, lax.rem(zed + step, n_rot)).astype(BF16)
            copy = pltpu.make_async_remote_copy(
                src_ref=outgoing.at[side, i],
                dst_ref=incoming.at[side, i],
                send_sem=e_send.at[side, i],
                recv_sem=e_recv.at[side, i],
                device_id=rot_peer(step),
                device_id_type=MESH,
            )
            copy.start()
            e_copies.append(copy)

    turn_references(0)
    send_partials(0)

    for copy in s_copies:
        copy.wait_recv()
    spread = spread_mine[...]
    for step in range(n_rot - 1):
        spread = spread + spread_in[step]
    root = each_row(jnp.sqrt(spread / K + 1e-6))
    for part in range(per_row):
        normed[zed, part] = (plain[part] / root).astype(BF16)
    r_copies = []
    for step in range(1, n_rot):
        r_copies.append(
            pltpu.make_async_remote_copy(
                src_ref=normed.at[zed],
                dst_ref=normed.at[zed],
                send_sem=r_send.at[step - 1],
                recv_sem=r_recv.at[step - 1],
                device_id=rot_peer(step),
                device_id_type=MESH,
            )
        )
        r_copies[-1].start()

    turn_references(1)
    send_partials(1)

    norm_mine[...] = square_rows[...].T[:8]
    n_copies = []
    for step in range(1, n_rot):
        n_copies.append(
            pltpu.make_async_remote_copy(
                src_ref=norm_mine,
                dst_ref=norm_in.at[step - 1],
                send_sem=n_send.at[step - 1],
                recv_sem=n_recv.at[step - 1],
                device_id=rot_peer(step),
                device_id_type=MESH,
            )
        )
        n_copies[-1].start()
    found = [partial(side, zed) for side in range(2)]

    for copy in r_copies:
        copy.wait_recv()
    for z in range(n_rot):
        for part in range(per_row):
            wide[0, part, :ROWS] = normed[z, part].astype(F32)
            for block in range(BLOCKS):
                first = (block // 4) * CYCLES * MFREQ + z * half
                first += (block % 4) * lanes + part * 128
                values = wide[0, part, pl.ds(block, CLS, stride=8), :]
                refs_ref[:, first : first + 128] = values.astype(BF16)

    for copy in n_copies:
        copy.wait_recv()
    spread = norm_mine[...]
    for step in range(n_rot - 1):
        spread = spread + norm_in[step]
    scale = (1.0 / math.sqrt(K)) / jnp.sqrt(spread / K + 1e-6)

    for side in range(2):
        whole = found[side]
        for i in range(n_rot - 1):
            e_copies[side * (n_rot - 1) + i].wait_recv()
            whole = whole + incoming[side, i].astype(F32)
        best = whole[:some]
        for fine in range(1, FINE):
            best = jnp.maximum(best, whole[fine * some : fine * some + some])
        square_rows[pl.ds(pl.multiple_of(halves[side] * some, 8), some), :] = best
    best = square_rows[...]
    best = best.T
    top = best[:share]
    for a in range(1, coarse):
        top = jnp.maximum(top, best[a * share : a * share + share])
    scores_ref[...] = top * scale[:1]

    for copy in sum(a_copies + c_copies, []) + s_copies + r_copies + e_copies + n_copies:
        copy.wait_send()


def trig_table(total):
    freqs = np.arange(128) % MFREQ
    phase = (np.arange(total)[:, None] * freqs[None, :]) % total * (2.0 * math.pi / total)
    return np.concatenate([np.cos(phase), np.sin(phase)], axis=1).astype(np.float32)


def local(n_dom, n_rot, particles, assign, rot_index, group, ctf_table):
    count = particles.shape[0]
    total = 8 * n_rot
    share = count // n_rot
    lanes = CYCLES // n_rot * MFREQ // 4
    half = 4 * lanes
    per_row = lanes // 128
    classes = CLS * n_dom
    vmem = pl.BlockSpec(memory_space=pltpu.VMEM)
    dma = pltpu.SemaphoreType.DMA
    sides = dma((2, n_dom // 2))
    parts, rot = dma((per_row, n_dom - 1)), dma((n_rot - 1,))
    shapes = (
        jax.ShapeDtypeStruct((CLS, K), BF16),
        jax.ShapeDtypeStruct((share, classes), F32),
    )
    return pl.pallas_call(
        functools.partial(kernel, n_dom, n_rot),
        out_shape=shapes,
        in_specs=[pl.BlockSpec(memory_space=pltpu.HBM)] * 6,
        out_specs=(vmem, vmem),
        scratch_shapes=[
            pltpu.VMEM((2, count, half), BF16),
            pltpu.VMEM((1, count), jnp.int32),
            pltpu.VMEM((1, count), jnp.int32),
            pltpu.VMEM((1, count), jnp.int32),
            pltpu.VMEM(ctf_table.shape, F32),
            pltpu.VMEM((total, 256), F32),
            pltpu.VMEM((per_row, n_dom * (ROWS + 8), 128), F32),
            pltpu.VMEM((n_dom - 1, per_row, ROWS + 8, 128), F32),
            pltpu.VMEM((n_dom, per_row, ROWS, 128), BF16),
            pltpu.VMEM((2, per_row, n_dom // 2 * ROWS, 128), F32),
            pltpu.VMEM((8, 128), F32),
            pltpu.VMEM((n_rot - 1, 8, 128), F32),
            pltpu.VMEM((n_rot, per_row, ROWS, 128), BF16),
            pltpu.VMEM((n_rot * 128, per_row * 1024), BF16),
            pltpu.VMEM((2, FINE * classes // 2, per_row * 1024), BF16),
            pltpu.VMEM((classes, 128), F32),
            pltpu.VMEM((2, n_rot - 1, FINE * classes // 2, 128), BF16),
            pltpu.VMEM((2, n_rot - 1, FINE * classes // 2, 128), BF16),
            pltpu.VMEM((8, classes), F32),
            pltpu.VMEM((n_rot - 1, 8, classes), F32),
            dma((7,)),
            parts, parts, sides, sides, rot, rot, rot, rot,
            dma((2, n_rot - 1)), dma((2, n_rot - 1)), rot, rot,
        ],
        compiler_params=pltpu.CompilerParams(
            collective_id=0, has_side_effects=True, vmem_limit_bytes=48 * 1024 * 1024
        ),
    )(
        *(
            pltpu.with_memory_space_constraint(x, pltpu.HBM)
            for x in (
                particles,
                assign.reshape(1, count),
                rot_index.reshape(1, count),
                group.reshape(1, count),
                ctf_table,
                jnp.asarray(trig_table(total)),
            )
        )
    )


def solution(mesh):
    sizes = dict(mesh.shape)
    in_specs = (P("dom", None), P("dom"), P("dom"), P("dom"), P())
    out_specs = (P("dom", None), P(("dom", "rot"), None))
    return jax.shard_map(
        functools.partial(local, sizes["dom"], sizes["rot"]),
        mesh=mesh, in_specs=in_specs, out_specs=out_specs, check_vma=False,
    )
```

```python
import functools
import math

import jax
import jax.numpy as jnp
import numpy as np
from jax import lax
from jax.experimental import pallas as pl
from jax.experimental.pallas import tpu as pltpu
from jax.sharding import PartitionSpec as P

CYCLES = 64
MFREQ = 64
CLS = 6
BLOCKS = 8
ROWS = BLOCKS * CLS
FINE = 4
K = 2 * CYCLES * MFREQ
MESH = pl.DeviceIdType.MESH
F32 = jnp.float32
BF16 = jnp.bfloat16


def pieces(x):
    high = x.astype(BF16)
    rest = x - high.astype(F32)
    mid = rest.astype(BF16)
    low = (rest - mid.astype(F32)).astype(BF16)
    return high, mid, low


def stacked(x):
    return jnp.concatenate(pieces(x), axis=0)


def iota(shape, dim):
    return lax.broadcasted_iota(jnp.int32, shape, dim)


def ones_where(cond):
    return jnp.where(cond, 1.0, 0.0).astype(BF16)


def dot(x, y):
    return jnp.dot(x, y, preferred_element_type=F32)


def column_onehot(row, count):
    shape = (3 * count, row.shape[1])
    return jnp.where((iota(shape, 0) & (count - 1)) == row, 1.0, 0.0).T.astype(BF16)


def each_row(tile):
    return jnp.concatenate([jnp.broadcast_to(tile[c : c + 1], (8, 128)) for c in range(CLS)], axis=0)


def kernel(
    n_dom, n_rot,
    particles_hbm, assign_hbm, rot_hbm, group_hbm, table_hbm, trig_hbm,
    refs_ref, scores_ref,
    spec, assign_ref, rot_ref, group_ref, table_ref, trig_ref,
    sums, sums_in, plain_all, wide, spread_mine, spread_in, normed, left, right,
    earlier, outgoing, incoming, norm_mine, norm_in,
    load_sem, a_send, a_recv, c_send, c_recv, s_send, s_recv, r_send, r_recv,
    e_send, e_recv, n_send, n_recv,
):
    me = lax.axis_index("dom")
    zed = lax.axis_index("rot")
    count = spec.shape[1]
    total = trig_ref.shape[0]
    share = count // n_rot
    coarse = total // FINE
    cyc = CYCLES // n_rot
    half = cyc * MFREQ
    lanes = half // 4
    per_row = lanes // 128
    classes = CLS * n_dom
    groups = table_ref.shape[0]

    barrier = pltpu.get_barrier_semaphore()

    def dom_peer(step):
        return (lax.rem(me + step, n_dom), zed)

    def rot_peer(step):
        return (me, lax.rem(zed + step, n_rot))

    for step in range(1, n_dom):
        pl.semaphore_signal(barrier, inc=1, device_id=dom_peer(step), device_id_type=MESH)
    for step in range(1, n_rot):
        pl.semaphore_signal(barrier, inc=1, device_id=rot_peer(step), device_id_type=MESH)

    pairs = [(group_hbm, group_ref), (table_hbm, table_ref), (rot_hbm, rot_ref)]
    pairs += [(trig_hbm, trig_ref), (assign_hbm, assign_ref)]
    for part in range(2):
        start = pl.multiple_of(part * CYCLES * MFREQ + zed * half, 128)
        pairs.append((particles_hbm.at[:, pl.ds(start, half)], spec.at[part]))
    loads = [pltpu.make_async_copy(x, y, load_sem.at[i]) for i, (x, y) in enumerate(pairs)]
    for load in loads:
        load.start()

    shape = (3 * CYCLES, half)
    spreader = ones_where((iota(shape, 0) & (CYCLES - 1)) == zed * cyc + iota(shape, 1) // MFREQ)
    loads[0].wait()
    loads[1].wait()
    rows = dot(column_onehot(group_ref[...], groups), stacked(table_ref[...]))
    factors = dot(jnp.concatenate(pieces(rows), axis=1), spreader)
    loads[2].wait()
    loads[3].wait()
    turns = dot(column_onehot(rot_ref[...], total), stacked(trig_ref[...]))
    cosine, sine = turns[:, :128], turns[:, 128:]

    loads[4].wait()
    labels = jnp.concatenate([assign_ref[...]] * 3, axis=1)
    place = iota((classes, 3 * count), 0)
    member = ones_where((place & (n_dom - 1)) * CLS + place // n_dom == labels)
    denom = dot(member, stacked(rows * rows))
    denom = jnp.concatenate([denom, jnp.zeros((classes, 128 - CYCLES), F32)], axis=1)
    for c in range(CLS):
        at = pl.ds(ROWS + c, n_dom, stride=ROWS + 8)
        sums[0, at, :] = denom[c * n_dom : c * n_dom + n_dom]

    def message(part, owner):
        first = pl.multiple_of(owner * (ROWS + 8), 8)
        return sums.at[part, pl.ds(first, ROWS + 8 if part == 0 else ROWS), :]

    def landing(part, step):
        return sums_in.at[step - 1, part, pl.ds(0, ROWS + 8 if part == 0 else ROWS), :]

    def lane_tile(block, part):
        first = block * lanes + part * 128
        return slice(first, first + 128)

    loads[5].wait()
    loads[6].wait()
    a_copies = []
    for part in range(per_row):
        for block in range(4):
            lane = lane_tile(block, part)
            re = spec[0, :, lane].astype(F32)
            im = spec[1, :, lane].astype(F32)
            both = [re * cosine + im * sine, im * cosine - re * sine]
            value = jnp.concatenate([x * factors[:, lane] for x in both], axis=1)
            numer = dot(member, stacked(value))
            for c in range(CLS):
                for i in range(2):
                    at = pl.ds(c * 8 + i * 4 + block, n_dom, stride=ROWS + 8)
                    sums[part, at, :] = numer[
                        c * n_dom : c * n_dom + n_dom, i * 128 : i * 128 + 128
                    ]
        if part == 0:
            pl.semaphore_wait(barrier, n_dom + n_rot - 2)
        group_copies = []
        for step in range(1, n_dom):
            group_copies.append(
                pltpu.make_async_remote_copy(
                    src_ref=message(part, lax.rem(me + step, n_dom)),
                    dst_ref=landing(part, step),
                    send_sem=a_send.at[part, step - 1],
                    recv_sem=a_recv.at[part, step - 1],
                    device_id=dom_peer(step),
                    device_id_type=MESH,
                )
            )
            group_copies[-1].start()
        a_copies.append(group_copies)

    steps = [n_rot // 2]
    for step in range(n_rot // 2 - 1, 0, -1):
        steps += [lax.select(zed % 2 == 0, n_rot - step, step)]
        steps += [lax.select(zed % 2 == 0, step, n_rot - step)]
    shape = (count, 128)
    spread_out = jnp.concatenate(
        [
            ones_where(
                iota(shape, 0) == lax.rem(zed + step, n_rot) * share + (iota(shape, 1) & (share - 1))
            )
            for step in steps + [0]
        ],
        axis=1,
    )
    shape = (3 * total, 128)
    picked = ones_where((iota(shape, 0) & (total - 1)) == iota(shape, 1) // share * FINE)
    over = (((0,), (0,)), ((), ()))
    table = stacked(trig_ref[...])
    cos_down = lax.dot_general(table[:, :128], picked, over, preferred_element_type=F32)
    sin_down = lax.dot_general(table[:, 128:], picked, over, preferred_element_type=F32)
    for part in range(per_row):
        for block in range(4):
            lane = lane_tile(block, part)
            re = (spec[0, :, lane].astype(F32) * factors[:, lane]).T.astype(BF16)
            im = (spec[1, :, lane].astype(F32) * factors[:, lane]).T.astype(BF16)
            for i in range(n_rot):
                at = slice(i * 128, i * 128 + 128)
                real = dot(re, spread_out[:, at])
                imag = dot(im, spread_out[:, at])
                first = block * 128
                left[part, first : first + 128, at] = (real * cos_down + imag * sin_down).astype(BF16)
                first = block * 128 + 512
                left[part, first : first + 128, at] = (imag * cos_down - real * sin_down).astype(BF16)

    cb = cyc // 4
    offset = iota((ROWS, 128), 1) - zed * cyc
    low = (iota((ROWS, 128), 0) & 3) * cb
    shape = (3 * 128, lanes)
    spreader = ones_where((iota(shape, 0) & (cb - 1)) == iota(shape, 1) // MFREQ)

    c_copies = []
    plain = []
    for part in range(per_row):
        for copy in a_copies[part]:
            copy.wait_recv()
        whole = message(part, me)[...]
        for step in range(1, n_dom):
            whole = whole + landing(part, step)[...]
        if part == 0:
            denom = jnp.where(
                (offset >= low) & (offset < low + cb), each_row(whole[ROWS:]), 0.0
            )
            denom = dot(jnp.concatenate(pieces(denom), axis=1), spreader) + 1.0
        plain.append(whole[:ROWS] / denom[:, part * 128 : part * 128 + 128])
        plain_all[part, me] = plain[-1].astype(BF16)
        group_copies = []
        for step in range(1, n_dom):
            group_copies.append(
                pltpu.make_async_remote_copy(
                    src_ref=plain_all.at[part, me],
                    dst_ref=plain_all.at[part, me],
                    send_sem=c_send.at[part, step - 1],
                    recv_sem=c_recv.at[part, step - 1],
                    device_id=dom_peer(step),
                    device_id_type=MESH,
                )
            )
            group_copies[-1].start()
        c_copies.append(group_copies)

    squares = sum(jnp.sum((x * x).reshape(CLS, 8, 128), axis=1) for x in plain)
    squares = jnp.broadcast_to(jnp.sum(squares, axis=1, keepdims=True), (CLS, 128))
    spread_mine[...] = jnp.concatenate([squares, jnp.zeros((8 - CLS, 128), F32)], axis=0)
    s_copies = []
    for step in range(1, n_rot):
        s_copies.append(
            pltpu.make_async_remote_copy(
                src_ref=spread_mine,
                dst_ref=spread_in.at[step - 1],
                send_sem=s_send.at[step - 1],
                recv_sem=s_recv.at[step - 1],
                device_id=rot_peer(step),
                device_id_type=MESH,
            )
        )
        s_copies[-1].start()

    def turn_references(part):
        for copy in c_copies[part]:
            copy.wait_recv()
        wide[part] = plain_all[part].astype(F32).reshape(classes * 8, 128)
        blocks = [wide[part, pl.ds(block, classes, stride=8), :] for block in range(BLOCKS)]
        for fine in range(FINE):
            cos = trig_ref[fine : fine + 1, :128]
            sin = trig_ref[fine : fine + 1, 128:]
            at = slice(fine * classes, fine * classes + classes)
            for block in range(4):
                re, im = blocks[block], blocks[block + 4]
                lane = slice(block * 128, block * 128 + 128)
                right[part, at, lane] = (re * cos - im * sin).astype(BF16)
                lane = slice(block * 128 + 512, block * 128 + 640)
                right[part, at, lane] = (re * sin + im * cos).astype(BF16)

    for part in range(per_row - 1):
        turn_references(part)
        found = dot(right[part], left[part])
        earlier[...] = found if part == 0 else earlier[...] + found

    for copy in s_copies:
        copy.wait_recv()
    spread = spread_mine[...]
    for step in range(n_rot - 1):
        spread = spread + spread_in[step]
    root = each_row(jnp.sqrt(spread / K + 1e-6))
    for part in range(per_row):
        normed[zed, part] = (plain[part] / root).astype(BF16)
    r_copies = []
    for step in range(1, n_rot):
        r_copies.append(
            pltpu.make_async_remote_copy(
                src_ref=normed.at[zed],
                dst_ref=normed.at[zed],
                send_sem=r_send.at[step - 1],
                recv_sem=r_recv.at[step - 1],
                device_id=rot_peer(step),
                device_id_type=MESH,
            )
        )
        r_copies[-1].start()

    last = per_row - 1
    turn_references(last)

    e_copies = []
    for pair in range(n_rot // 2):
        at = slice(pair * 256, pair * 256 + 256)
        found = dot(right[last], left[last, :, at])
        if last:
            found = found + earlier[:, at]
        for i in range(2 * pair, min(2 * pair + 2, n_rot - 1)):
            outgoing[i] = found[:, (i % 2) * 128 : (i % 2) * 128 + 128].astype(BF16)
            e_copies.append(
                pltpu.make_async_remote_copy(
                    src_ref=outgoing.at[i],
                    dst_ref=incoming.at[i],
                    send_sem=e_send.at[i],
                    recv_sem=e_recv.at[i],
                    device_id=rot_peer(steps[i]),
                    device_id_type=MESH,
                )
            )
            e_copies[-1].start()
    found = found[:, 128:]

    squares = jnp.zeros((classes, 128), F32)
    for part in range(per_row):
        for block in range(BLOCKS):
            x = wide[part, pl.ds(block, classes, stride=8), :]
            squares = squares + x * x
    squares = jnp.broadcast_to(jnp.sum(squares, axis=1, keepdims=True), (classes, 128))
    norm_mine[...] = squares.T[:8]
    n_copies = []
    for step in range(1, n_rot):
        n_copies.append(
            pltpu.make_async_remote_copy(
                src_ref=norm_mine,
                dst_ref=norm_in.at[step - 1],
                send_sem=n_send.at[step - 1],
                recv_sem=n_recv.at[step - 1],
                device_id=rot_peer(step),
                device_id_type=MESH,
            )
        )
        n_copies[-1].start()

    for copy in r_copies:
        copy.wait_recv()
    for z in range(n_rot):
        for part in range(per_row):
            wide[part, :ROWS] = normed[z, part].astype(F32)
            for block in range(BLOCKS):
                first = (block // 4) * CYCLES * MFREQ + z * half
                first += (block % 4) * lanes + part * 128
                values = wide[part, pl.ds(block, CLS, stride=8), :]
                refs_ref[:, first : first + 128] = values.astype(BF16)

    for copy in n_copies:
        copy.wait_recv()
    spread = norm_mine[...]
    for step in range(n_rot - 1):
        spread = spread + norm_in[step]
    scale = (1.0 / math.sqrt(K)) / jnp.sqrt(spread / K + 1e-6)

    for i, copy in enumerate(e_copies):
        copy.wait_recv()
        found = found + incoming[i].astype(F32)
    best = found[:classes]
    for fine in range(1, FINE):
        best = jnp.maximum(best, found[fine * classes : fine * classes + classes])
    best = best.T
    top = best[:share]
    for a in range(1, coarse):
        top = jnp.maximum(top, best[a * share : a * share + share])
    scores_ref[...] = top * scale[:1]

    for copy in sum(a_copies + c_copies, []) + s_copies + r_copies + e_copies + n_copies:
        copy.wait_send()


def trig_table(total):
    freqs = np.arange(128) % MFREQ
    phase = (np.arange(total)[:, None] * freqs[None, :]) % total * (2.0 * math.pi / total)
    return np.concatenate([np.cos(phase), np.sin(phase)], axis=1).astype(np.float32)


def local(n_dom, n_rot, particles, assign, rot_index, group, ctf_table):
    count = particles.shape[0]
    total = 8 * n_rot
    share = count // n_rot
    lanes = CYCLES // n_rot * MFREQ // 4
    half = 4 * lanes
    per_row = lanes // 128
    classes = CLS * n_dom
    vmem = pl.BlockSpec(memory_space=pltpu.VMEM)
    dma = pltpu.SemaphoreType.DMA
    parts, rot = dma((per_row, n_dom - 1)), dma((n_rot - 1,))
    shapes = (
        jax.ShapeDtypeStruct((CLS, K), BF16),
        jax.ShapeDtypeStruct((share, classes), F32),
    )
    return pl.pallas_call(
        functools.partial(kernel, n_dom, n_rot),
        out_shape=shapes,
        in_specs=[pl.BlockSpec(memory_space=pltpu.HBM)] * 6,
        out_specs=(vmem, vmem),
        scratch_shapes=[
            pltpu.VMEM((2, count, half), BF16),
            pltpu.VMEM((1, count), jnp.int32),
            pltpu.VMEM((1, count), jnp.int32),
            pltpu.VMEM((1, count), jnp.int32),
            pltpu.VMEM(ctf_table.shape, F32),
            pltpu.VMEM((total, 256), F32),
            pltpu.VMEM((per_row, n_dom * (ROWS + 8), 128), F32),
            pltpu.VMEM((n_dom - 1, per_row, ROWS + 8, 128), F32),
            pltpu.VMEM((per_row, n_dom, ROWS, 128), BF16),
            pltpu.VMEM((per_row, n_dom * ROWS, 128), F32),
            pltpu.VMEM((8, 128), F32),
            pltpu.VMEM((n_rot - 1, 8, 128), F32),
            pltpu.VMEM((n_rot, per_row, ROWS, 128), BF16),
            pltpu.VMEM((per_row, 1024, n_rot * 128), BF16),
            pltpu.VMEM((per_row, FINE * classes, 1024), BF16),
            pltpu.VMEM((FINE * classes, n_rot * 128), F32),
            pltpu.VMEM((n_rot - 1, FINE * classes, 128), BF16),
            pltpu.VMEM((n_rot - 1, FINE * classes, 128), BF16),
            pltpu.VMEM((8, classes), F32),
            pltpu.VMEM((n_rot - 1, 8, classes), F32),
            dma((7,)),
            parts, parts, parts, parts, rot, rot, rot, rot, rot, rot, rot, rot,
        ],
        compiler_params=pltpu.CompilerParams(
            collective_id=0, has_side_effects=True, vmem_limit_bytes=48 * 1024 * 1024
        ),
    )(
        *(
            pltpu.with_memory_space_constraint(x, pltpu.HBM)
            for x in (
                particles,
                assign.reshape(1, count),
                rot_index.reshape(1, count),
                group.reshape(1, count),
                ctf_table,
                jnp.asarray(trig_table(total)),
            )
        )
    )


def solution(mesh):
    sizes = dict(mesh.shape)
    in_specs = (P("dom", None), P("dom"), P("dom"), P("dom"), P())
    out_specs = (P("dom", None), P(("dom", "rot"), None))
    return jax.shard_map(
        functools.partial(local, sizes["dom"], sizes["rot"]),
        mesh=mesh, in_specs=in_specs, out_specs=out_specs, check_vma=False,
    )
```

```python
import functools
import math

import jax
import jax.numpy as jnp
import numpy as np
from jax import lax
from jax.experimental import pallas as pl
from jax.experimental.pallas import tpu as pltpu
from jax.sharding import PartitionSpec as P

CYCLES = 64
MFREQ = 64
CLS = 6
BLOCKS = 8
ROWS = BLOCKS * CLS
FINE = 4
K = 2 * CYCLES * MFREQ
MESH = pl.DeviceIdType.MESH
F32 = jnp.float32
BF16 = jnp.bfloat16


def pieces(x):
    high = x.astype(BF16)
    rest = x - high.astype(F32)
    mid = rest.astype(BF16)
    low = (rest - mid.astype(F32)).astype(BF16)
    return high, mid, low


def stacked(x):
    return jnp.concatenate(pieces(x), axis=0)


def iota(shape, dim):
    return lax.broadcasted_iota(jnp.int32, shape, dim)


def ones_where(cond):
    return jnp.where(cond, 1.0, 0.0).astype(BF16)


def dot(x, y):
    return jnp.dot(x, y, preferred_element_type=F32)


def column_onehot(row, count):
    shape = (3 * count, row.shape[1])
    return jnp.where((iota(shape, 0) & (count - 1)) == row, 1.0, 0.0).T.astype(BF16)


def each_row(tile):
    return jnp.concatenate([jnp.broadcast_to(tile[c : c + 1], (8, 128)) for c in range(CLS)], axis=0)


def kernel(
    n_dom, n_rot,
    particles_hbm, assign_hbm, rot_hbm, group_hbm, table_hbm, trig_hbm,
    refs_ref, scores_ref,
    spec, assign_ref, rot_ref, group_ref, table_ref, trig_ref,
    sums, sums_in, plain_all, wide, spread_mine, spread_in, normed, left, right,
    earlier, outgoing, incoming, norm_mine, norm_in,
    load_sem, a_send, a_recv, c_send, c_recv, s_send, s_recv, r_send, r_recv,
    e_send, e_recv, n_send, n_recv,
):
    me = lax.axis_index("dom")
    zed = lax.axis_index("rot")
    count = spec.shape[1]
    total = trig_ref.shape[0]
    share = count // n_rot
    coarse = total // FINE
    cyc = CYCLES // n_rot
    half = cyc * MFREQ
    lanes = half // 4
    per_row = lanes // 128
    classes = CLS * n_dom
    groups = table_ref.shape[0]

    barrier = pltpu.get_barrier_semaphore()

    def dom_peer(step):
        return (lax.rem(me + step, n_dom), zed)

    def rot_peer(step):
        return (me, lax.rem(zed + step, n_rot))

    pairs = [(group_hbm, group_ref), (table_hbm, table_ref), (rot_hbm, rot_ref)]
    pairs += [(trig_hbm, trig_ref), (assign_hbm, assign_ref)]
    for part in range(2):
        start = pl.multiple_of(part * CYCLES * MFREQ + zed * half, 128)
        pairs.append((particles_hbm.at[:, pl.ds(start, half)], spec.at[part]))
    loads = [pltpu.make_async_copy(x, y, load_sem.at[i]) for i, (x, y) in enumerate(pairs)]
    for load in loads:
        load.start()

    for step in range(1, n_dom):
        pl.semaphore_signal(barrier, inc=1, device_id=dom_peer(step), device_id_type=MESH)
    for step in range(1, n_rot):
        pl.semaphore_signal(barrier, inc=1, device_id=rot_peer(step), device_id_type=MESH)

    shape = (3 * CYCLES, half)
    spreader = ones_where((iota(shape, 0) & (CYCLES - 1)) == zed * cyc + iota(shape, 1) // MFREQ)
    loads[0].wait()
    loads[1].wait()
    rows = dot(column_onehot(group_ref[...], groups), stacked(table_ref[...]))
    factors = dot(jnp.concatenate(pieces(rows), axis=1), spreader)
    loads[2].wait()
    loads[3].wait()
    turns = dot(column_onehot(rot_ref[...], total), stacked(trig_ref[...]))
    cosine, sine = turns[:, :128], turns[:, 128:]

    loads[4].wait()
    labels = jnp.concatenate([assign_ref[...]] * 3, axis=1)
    place = iota((classes, 3 * count), 0)
    member = ones_where((place & (n_dom - 1)) * CLS + place // n_dom == labels)
    denom = dot(member, stacked(rows * rows))
    denom = jnp.concatenate([denom, jnp.zeros((classes, 128 - CYCLES), F32)], axis=1)
    for c in range(CLS):
        at = pl.ds(ROWS + c, n_dom, stride=ROWS + 8)
        sums[0, at, :] = denom[c * n_dom : c * n_dom + n_dom]

    def message(part, owner):
        first = pl.multiple_of(owner * (ROWS + 8), 8)
        return sums.at[part, pl.ds(first, ROWS + 8 if part == 0 else ROWS), :]

    def landing(part, step):
        return sums_in.at[step - 1, part, pl.ds(0, ROWS + 8 if part == 0 else ROWS), :]

    def lane_tile(block, part):
        first = block * lanes + part * 128
        return slice(first, first + 128)

    loads[5].wait()
    loads[6].wait()
    a_copies = []
    for part in range(per_row):
        for block in range(4):
            lane = lane_tile(block, part)
            re = spec[0, :, lane].astype(F32)
            im = spec[1, :, lane].astype(F32)
            both = [re * cosine + im * sine, im * cosine - re * sine]
            value = jnp.concatenate([x * factors[:, lane] for x in both], axis=1)
            numer = dot(member, stacked(value))
            for c in range(CLS):
                for i in range(2):
                    at = pl.ds(c * 8 + i * 4 + block, n_dom, stride=ROWS + 8)
                    sums[part, at, :] = numer[
                        c * n_dom : c * n_dom + n_dom, i * 128 : i * 128 + 128
                    ]
        if part == 0:
            pl.semaphore_wait(barrier, n_dom + n_rot - 2)
        group_copies = []
        for step in range(1, n_dom):
            group_copies.append(
                pltpu.make_async_remote_copy(
                    src_ref=message(part, lax.rem(me + step, n_dom)),
                    dst_ref=landing(part, step),
                    send_sem=a_send.at[part, step - 1],
                    recv_sem=a_recv.at[part, step - 1],
                    device_id=dom_peer(step),
                    device_id_type=MESH,
                )
            )
            group_copies[-1].start()
        a_copies.append(group_copies)

    steps = [n_rot // 2]
    for step in range(n_rot // 2 - 1, 0, -1):
        steps += [lax.select(zed % 2 == 0, n_rot - step, step)]
        steps += [lax.select(zed % 2 == 0, step, n_rot - step)]
    shape = (count, 128)
    spread_out = jnp.concatenate(
        [
            ones_where(
                iota(shape, 0) == lax.rem(zed + step, n_rot) * share + (iota(shape, 1) & (share - 1))
            )
            for step in steps + [0]
        ],
        axis=1,
    )
    shape = (3 * total, 128)
    picked = ones_where((iota(shape, 0) & (total - 1)) == iota(shape, 1) // share * FINE)
    over = (((0,), (0,)), ((), ()))
    table = stacked(trig_ref[...])
    cos_down = lax.dot_general(table[:, :128], picked, over, preferred_element_type=F32)
    sin_down = lax.dot_general(table[:, 128:], picked, over, preferred_element_type=F32)
    for part in range(per_row):
        for block in range(4):
            lane = lane_tile(block, part)
            re = (spec[0, :, lane].astype(F32) * factors[:, lane]).T.astype(BF16)
            im = (spec[1, :, lane].astype(F32) * factors[:, lane]).T.astype(BF16)
            for i in range(n_rot):
                at = slice(i * 128, i * 128 + 128)
                real = dot(re, spread_out[:, at])
                imag = dot(im, spread_out[:, at])
                first = block * 128
                left[part, first : first + 128, at] = (real * cos_down + imag * sin_down).astype(BF16)
                first = block * 128 + 512
                left[part, first : first + 128, at] = (imag * cos_down - real * sin_down).astype(BF16)

    cb = cyc // 4
    offset = iota((ROWS, 128), 1) - zed * cyc
    low = (iota((ROWS, 128), 0) & 3) * cb
    shape = (3 * 128, lanes)
    spreader = ones_where((iota(shape, 0) & (cb - 1)) == iota(shape, 1) // MFREQ)

    c_copies = []
    plain = []
    for part in range(per_row):
        for copy in a_copies[part]:
            copy.wait_recv()
        whole = message(part, me)[...]
        for step in range(1, n_dom):
            whole = whole + landing(part, step)[...]
        if part == 0:
            denom = jnp.where(
                (offset >= low) & (offset < low + cb), each_row(whole[ROWS:]), 0.0
            )
            denom = dot(jnp.concatenate(pieces(denom), axis=1), spreader) + 1.0
        plain.append(whole[:ROWS] / denom[:, part * 128 : part * 128 + 128])
        plain_all[part, me] = plain[-1].astype(BF16)
        group_copies = []
        for step in range(1, n_dom):
            group_copies.append(
                pltpu.make_async_remote_copy(
                    src_ref=plain_all.at[part, me],
                    dst_ref=plain_all.at[part, me],
                    send_sem=c_send.at[part, step - 1],
                    recv_sem=c_recv.at[part, step - 1],
                    device_id=dom_peer(step),
                    device_id_type=MESH,
                )
            )
            group_copies[-1].start()
        c_copies.append(group_copies)

    squares = sum(jnp.sum((x * x).reshape(CLS, 8, 128), axis=1) for x in plain)
    squares = jnp.broadcast_to(jnp.sum(squares, axis=1, keepdims=True), (CLS, 128))
    spread_mine[...] = jnp.concatenate([squares, jnp.zeros((8 - CLS, 128), F32)], axis=0)
    s_copies = []
    for step in range(1, n_rot):
        s_copies.append(
            pltpu.make_async_remote_copy(
                src_ref=spread_mine,
                dst_ref=spread_in.at[step - 1],
                send_sem=s_send.at[step - 1],
                recv_sem=s_recv.at[step - 1],
                device_id=rot_peer(step),
                device_id_type=MESH,
            )
        )
        s_copies[-1].start()

    def turn_references(part):
        for copy in c_copies[part]:
            copy.wait_recv()
        wide[part] = plain_all[part].astype(F32).reshape(classes * 8, 128)
        blocks = [wide[part, pl.ds(block, classes, stride=8), :] for block in range(BLOCKS)]
        for fine in range(FINE):
            cos = trig_ref[fine : fine + 1, :128]
            sin = trig_ref[fine : fine + 1, 128:]
            at = slice(fine * classes, fine * classes + classes)
            for block in range(4):
                re, im = blocks[block], blocks[block + 4]
                lane = slice(block * 128, block * 128 + 128)
                right[part, at, lane] = (re * cos - im * sin).astype(BF16)
                lane = slice(block * 128 + 512, block * 128 + 640)
                right[part, at, lane] = (re * sin + im * cos).astype(BF16)

    for part in range(per_row - 1):
        turn_references(part)
        found = dot(right[part], left[part])
        earlier[...] = found if part == 0 else earlier[...] + found

    for copy in s_copies:
        copy.wait_recv()
    spread = spread_mine[...]
    for step in range(n_rot - 1):
        spread = spread + spread_in[step]
    root = each_row(jnp.sqrt(spread / K + 1e-6))
    for part in range(per_row):
        normed[zed, part] = (plain[part] / root).astype(BF16)
    r_copies = []
    for step in range(1, n_rot):
        r_copies.append(
            pltpu.make_async_remote_copy(
                src_ref=normed.at[zed],
                dst_ref=normed.at[zed],
                send_sem=r_send.at[step - 1],
                recv_sem=r_recv.at[step - 1],
                device_id=rot_peer(step),
                device_id_type=MESH,
            )
        )
        r_copies[-1].start()

    last = per_row - 1
    turn_references(last)

    e_copies = []
    for pair in range(n_rot // 2):
        at = slice(pair * 256, pair * 256 + 256)
        found = dot(right[last], left[last, :, at])
        if last:
            found = found + earlier[:, at]
        for i in range(2 * pair, min(2 * pair + 2, n_rot - 1)):
            outgoing[i] = found[:, (i % 2) * 128 : (i % 2) * 128 + 128].astype(BF16)
            e_copies.append(
                pltpu.make_async_remote_copy(
                    src_ref=outgoing.at[i],
                    dst_ref=incoming.at[i],
                    send_sem=e_send.at[i],
                    recv_sem=e_recv.at[i],
                    device_id=rot_peer(steps[i]),
                    device_id_type=MESH,
                )
            )
            e_copies[-1].start()
    found = found[:, 128:]

    squares = jnp.zeros((classes, 128), F32)
    for part in range(per_row):
        for block in range(BLOCKS):
            x = wide[part, pl.ds(block, classes, stride=8), :]
            squares = squares + x * x
    squares = jnp.broadcast_to(jnp.sum(squares, axis=1, keepdims=True), (classes, 128))
    norm_mine[...] = squares.T[:8]
    n_copies = []
    for step in range(1, n_rot):
        n_copies.append(
            pltpu.make_async_remote_copy(
                src_ref=norm_mine,
                dst_ref=norm_in.at[step - 1],
                send_sem=n_send.at[step - 1],
                recv_sem=n_recv.at[step - 1],
                device_id=rot_peer(step),
                device_id_type=MESH,
            )
        )
        n_copies[-1].start()

    for copy in r_copies:
        copy.wait_recv()
    for z in range(n_rot):
        for part in range(per_row):
            wide[part, :ROWS] = normed[z, part].astype(F32)
            for block in range(BLOCKS):
                first = (block // 4) * CYCLES * MFREQ + z * half
                first += (block % 4) * lanes + part * 128
                values = wide[part, pl.ds(block, CLS, stride=8), :]
                refs_ref[:, first : first + 128] = values.astype(BF16)

    for copy in n_copies:
        copy.wait_recv()
    spread = norm_mine[...]
    for step in range(n_rot - 1):
        spread = spread + norm_in[step]
    scale = (1.0 / math.sqrt(K)) / jnp.sqrt(spread / K + 1e-6)

    for i, copy in enumerate(e_copies):
        copy.wait_recv()
        found = found + incoming[i].astype(F32)
    best = found[:classes]
    for fine in range(1, FINE):
        best = jnp.maximum(best, found[fine * classes : fine * classes + classes])
    best = best.T
    top = best[:share]
    for a in range(1, coarse):
        top = jnp.maximum(top, best[a * share : a * share + share])
    scores_ref[...] = top * scale[:1]

    for copy in sum(a_copies + c_copies, []) + s_copies + r_copies + e_copies + n_copies:
        copy.wait_send()


def trig_table(total):
    freqs = np.arange(128) % MFREQ
    phase = (np.arange(total)[:, None] * freqs[None, :]) % total * (2.0 * math.pi / total)
    return np.concatenate([np.cos(phase), np.sin(phase)], axis=1).astype(np.float32)


def local(n_dom, n_rot, particles, assign, rot_index, group, ctf_table):
    count = particles.shape[0]
    total = 8 * n_rot
    share = count // n_rot
    lanes = CYCLES // n_rot * MFREQ // 4
    half = 4 * lanes
    per_row = lanes // 128
    classes = CLS * n_dom
    vmem = pl.BlockSpec(memory_space=pltpu.VMEM)
    dma = pltpu.SemaphoreType.DMA
    parts, rot = dma((per_row, n_dom - 1)), dma((n_rot - 1,))
    shapes = (
        jax.ShapeDtypeStruct((CLS, K), BF16),
        jax.ShapeDtypeStruct((share, classes), F32),
    )
    return pl.pallas_call(
        functools.partial(kernel, n_dom, n_rot),
        out_shape=shapes,
        in_specs=[pl.BlockSpec(memory_space=pltpu.HBM)] * 6,
        out_specs=(vmem, vmem),
        scratch_shapes=[
            pltpu.VMEM((2, count, half), BF16),
            pltpu.VMEM((1, count), jnp.int32),
            pltpu.VMEM((1, count), jnp.int32),
            pltpu.VMEM((1, count), jnp.int32),
            pltpu.VMEM(ctf_table.shape, F32),
            pltpu.VMEM((total, 256), F32),
            pltpu.VMEM((per_row, n_dom * (ROWS + 8), 128), F32),
            pltpu.VMEM((n_dom - 1, per_row, ROWS + 8, 128), F32),
            pltpu.VMEM((per_row, n_dom, ROWS, 128), BF16),
            pltpu.VMEM((per_row, n_dom * ROWS, 128), F32),
            pltpu.VMEM((8, 128), F32),
            pltpu.VMEM((n_rot - 1, 8, 128), F32),
            pltpu.VMEM((n_rot, per_row, ROWS, 128), BF16),
            pltpu.VMEM((per_row, 1024, n_rot * 128), BF16),
            pltpu.VMEM((per_row, FINE * classes, 1024), BF16),
            pltpu.VMEM((FINE * classes, n_rot * 128), F32),
            pltpu.VMEM((n_rot - 1, FINE * classes, 128), BF16),
            pltpu.VMEM((n_rot - 1, FINE * classes, 128), BF16),
            pltpu.VMEM((8, classes), F32),
            pltpu.VMEM((n_rot - 1, 8, classes), F32),
            dma((7,)),
            parts, parts, parts, parts, rot, rot, rot, rot, rot, rot, rot, rot,
        ],
        compiler_params=pltpu.CompilerParams(
            collective_id=0, has_side_effects=True, vmem_limit_bytes=48 * 1024 * 1024
        ),
    )(
        *(
            pltpu.with_memory_space_constraint(x, pltpu.HBM)
            for x in (
                particles,
                assign.reshape(1, count),
                rot_index.reshape(1, count),
                group.reshape(1, count),
                ctf_table,
                jnp.asarray(trig_table(total)),
            )
        )
    )


def solution(mesh):
    sizes = dict(mesh.shape)
    in_specs = (P("dom", None), P("dom"), P("dom"), P("dom"), P())
    out_specs = (P("dom", None), P(("dom", "rot"), None))
    return jax.shard_map(
        functools.partial(local, sizes["dom"], sizes["rot"]),
        mesh=mesh, in_specs=in_specs, out_specs=out_specs, check_vma=False,
    )
```
